32 devices in a mesh: op: 4 (over y, x), sec: 8 (over z, core).
Axes of the slice: x: 2, y: 2, z: 4, core: 2. Of those that a mesh axis runs over, the one named last changes fastest.
Arguments:
- wavefunction: bfloat16 [512, 128, 128], P('sec'), may hold values from -6 to 6
- left_ops: bfloat16 [2, 16, 8, 128, 128], P(None, 'op'), may hold values from -0.5 to 0.5
- right_ops: bfloat16 [2, 16, 8, 128, 128], P(None, 'op'), may hold values from -0.09375 to 0.09375
- left_sector: int32 [512], P('sec'), may hold values from 0 to 7
- right_sector: int32 [512], P('sec'), may hold values from 0 to 7
- target: int32 [2, 512], replicated, may hold values from 0 to 511, as said below
Outputs:
- applied_blocks: float32 [512, 128, 128], P('sec', 'op')
The draws below stay inside these ranges and needn't reach their ends.
Inputs may be any that keep to these rules, and one draw needn't show every extreme that they name: For every class, target is a permutation of the 512 blocks; block b lies on index b // 64 of sec, and for every class exactly 8 of the blocks of one index of sec map to blocks of each index of sec.
All inputs are finite; a program needn't handle non-finite values.
Results may differ from the reference program's by a relative error of at most 0.0029.
Values may be sent and summed in bfloat16 or wider, within the bound.
A program may use at most 64 MiB of HBM per device.

```python
import jax
import jax.numpy as jnp
from jax import lax

BL = 128
BR = 128
NL = 8
NR = 8
CLASSES = 2
BLOCK_DEV = 64
TERMS = 16
BLOCKS = 512


def draw_target(key, part):
    shards = BLOCKS // BLOCK_DEV
    rows_out = []
    for class_index in range(CLASSES):
        keys = jax.random.split(jax.random.fold_in(key, 7001 + class_index), 3)
        device_perm = jax.random.permutation(keys[0], shards)
        offset_perm = jax.random.permutation(keys[1], shards)
        slot_perm = jax.random.permutation(keys[2], BLOCK_DEV)
        device_ids = jnp.arange(shards, dtype=jnp.int32)[:, None]
        slot_ids = jnp.arange(BLOCK_DEV, dtype=jnp.int32)[None, :]
        dest_device = (device_perm[device_ids] + offset_perm[slot_ids % shards]) % shards
        mapped = dest_device * BLOCK_DEV + slot_perm[slot_ids]
        rows_out.append(mapped.reshape(-1))
    return jnp.stack(rows_out).astype(jnp.int32)


def plant(array, stream_key, low, high):
    extent = array.shape
    index_at = [jax.random.randint(jax.random.fold_in(stream_key, axis), (), 0, extent[axis]) for axis in range(len(extent))]
    array = array.at[tuple(index_at)].set(low)
    longest = extent.index(max(extent))
    index_at[longest] = (index_at[longest] + 1) % extent[longest]
    return array.at[tuple(index_at)].set(high)


def level_of(stream_key, extent, pieces, smallest, top_value):
    factor_of, own = 1.0, jax.random.fold_in(stream_key, 6)
    for axis_at, parts in pieces:
        steps = jnp.exp(jax.random.uniform(jax.random.fold_in(own, axis_at), (parts,), jnp.float32, smallest / len(pieces), top_value / len(pieces)))
        factor_of = factor_of * jnp.repeat(steps, extent[axis_at] // parts).reshape([-1 if axis == axis_at else 1 for axis in range(len(extent))])
    return factor_of


def scatter_about(stream_key, shape, scale, bound, cuts=(), held_as=jnp.bfloat16):
    entries = scale * jax.random.normal(stream_key, shape, jnp.float32)
    if cuts:
        entries = entries * level_of(stream_key, shape, cuts, -0.22, 0.18)
    return jnp.clip(entries, -bound, bound).astype(held_as)


def setup_inputs(seed: int = 0) -> dict:
    key_of = jax.random.split(jax.random.key(seed), 7)
    wavefunction = scatter_about(key_of[0], (BLOCKS, BL, BR), 1.0, 6.0, ((0, 8),))
    left_ops = scatter_about(key_of[1], (CLASSES, TERMS, NL, BL, BL), BL ** -0.5, 0.5, ((1, 4),))
    right_ops = scatter_about(key_of[2], (CLASSES, TERMS, NR, BR, BR), (BR * CLASSES * TERMS) ** -0.5, 0.09375, ((1, 4),))
    left_sector = plant(jax.random.randint(key_of[3], (BLOCKS,), 0, NL), jax.random.fold_in(key_of[3], 1), 0, NL - 1).astype(jnp.int32)
    right_sector = plant(jax.random.randint(key_of[4], (BLOCKS,), 0, NR), jax.random.fold_in(key_of[4], 1), 0, NR - 1).astype(jnp.int32)
    target = draw_target(jax.random.fold_in(key_of[6], 71), 0)
    return {"wavefunction": wavefunction, "left_ops": left_ops, "right_ops": right_ops, "left_sector": left_sector, "right_sector": right_sector, "target": target}


def reference(wavefunction, left_ops, right_ops, left_sector, right_sector, target):
    wave_float = wavefunction.astype(jnp.float32)
    applied = jnp.zeros(wavefunction.shape, jnp.float32)
    for class_index in range(CLASSES):
        def term_step(running, operators):
            left_term, right_term = operators
            left_blocks = jnp.take(left_term, left_sector, axis=0).astype(jnp.float32)
            right_blocks = jnp.take(right_term, right_sector, axis=0).astype(jnp.float32)
            mixed = jnp.einsum("bij,bjk->bik", left_blocks, wave_float).astype(jnp.bfloat16)
            mixed = lax.optimization_barrier(mixed).astype(jnp.float32)
            return running + jnp.einsum("bik,blk->bil", mixed, right_blocks), None

        initial = jnp.zeros(wavefunction.shape, jnp.float32)
        running, _ = lax.scan(term_step, initial, (left_ops[class_index], right_ops[class_index]))
        applied = applied.at[target[class_index]].add(running)
    return applied
```

```python
import functools

import jax
import jax.numpy as jnp
from jax import lax
from jax.experimental import pallas as pl
from jax.experimental.pallas import tpu as pltpu
from jax.sharding import PartitionSpec as P

MESH = pl.DeviceIdType.MESH
GROUP = 8
LAG_SECOND = 1
LAG_ROUTE = 2


def kernel(sizes, left_sm, right_sm, send_sm, recv_sm, w_ref, l_ref, r_ref, out_ref,
           acc, s1, r1, s2, r2, s3, arr, sem_s1, sem_r1, sem_s2, sem_r2, sem_s3, sem_r3):
    shards, classes, chunks, chunk, slots = sizes
    half = chunk // 2
    terms, bl = l_ref.shape[1], l_ref.shape[3]
    rows = acc.shape[3]
    op, me = lax.axis_index("op"), lax.axis_index("sec")
    hi, lo = op // 2, op % 2
    own = hi * 2 + lo
    near_lo, near_hi = hi * 2 + 1 - lo, (1 - hi) * 2 + lo
    dests = chunk // slots

    def peer(k):
        off = shards // 2 + (1 - 2 * (k % 2)) * ((k + 1) // 2)
        return (me + off + shards) % shards

    barrier = pltpu.get_barrier_semaphore()
    for other in (near_lo, near_hi):
        pl.semaphore_signal(barrier, inc=1, device_id={"op": other}, device_id_type=MESH)

    def greet(k, carry):
        pl.semaphore_signal(barrier, inc=1, device_id={"sec": peer(k)}, device_id_type=MESH)
        return carry

    lax.fori_loop(0, shards - 1, greet, 0)
    pl.semaphore_wait(barrier, 2 + shards - 1)

    def first_copy(h, i):
        return pltpu.make_async_remote_copy(
            src_ref=s1.at[h, i], dst_ref=r1.at[h, i], send_sem=sem_s1.at[h, i], recv_sem=sem_r1.at[h, i],
            device_id={"op": near_lo if h == 0 else near_hi}, device_id_type=MESH)

    def second_copy(h, i):
        return pltpu.make_async_remote_copy(
            src_ref=s2.at[h, i], dst_ref=r2.at[h, i], send_sem=sem_s2.at[h, i], recv_sem=sem_r2.at[h, i],
            device_id={"op": near_hi if h == 0 else near_lo}, device_id_type=MESH)

    def route_copy(i, e, q, k):
        return pltpu.make_async_remote_copy(
            src_ref=s3.at[i, e], dst_ref=arr.at[q, me], send_sem=sem_s3.at[i, e], recv_sem=sem_r3.at[q, me],
            device_id={"sec": peer(k)}, device_id_type=MESH)

    def compute(i):
        q, c = i % classes, i // classes
        for b in range(chunk):
            dest = peer(c * dests + b // slots)
            block = send_sm[q, dest * slots + b % slots]
            left = left_sm[block]
            right = right_sm[block]
            mixed = jnp.dot(
                l_ref[q, :, left].reshape(terms * bl, l_ref.shape[4]), w_ref[block],
                preferred_element_type=jnp.float32).astype(jnp.bfloat16)
            mixed = jnp.concatenate([mixed[t * bl:(t + 1) * bl] for t in range(terms)], axis=1)
            rights = jnp.concatenate([r_ref[q, t, right] for t in range(terms)], axis=1)
            value = lax.dot_general(mixed, rights, (((1,), (1,)), ((), ())), preferred_element_type=jnp.float32)
            acc[i, b] = value.reshape(acc.shape[2:])
        for j in range(2):
            s1[0, i, :, j] = acc[i, 0:half, j * 2 + 1 - lo].astype(jnp.bfloat16)
        first_copy(0, i).start()
        for j in range(2):
            s1[1, i, :, j] = acc[i, half:chunk, (1 - hi) * 2 + j].astype(jnp.bfloat16)
        first_copy(1, i).start()

    def second(i):
        first_copy(0, i).wait_recv()
        s2[0, i] = (acc[i, 0:half, near_hi] + r1[0, i, :, 1 - hi].astype(jnp.float32)).astype(jnp.bfloat16)
        second_copy(0, i).start()
        first_copy(1, i).wait_recv()
        s2[1, i] = (acc[i, half:chunk, near_lo] + r1[1, i, :, 1 - lo].astype(jnp.float32)).astype(jnp.bfloat16)
        second_copy(1, i).start()
        acc[i, 0:half, own] = acc[i, 0:half, own] + r1[0, i, :, hi].astype(jnp.float32)
        acc[i, half:chunk, own] = acc[i, half:chunk, own] + r1[1, i, :, lo].astype(jnp.float32)

    def route(i):
        q, c = i % classes, i // classes
        for h in range(2):
            second_copy(h, i).wait_recv()
            total = acc[i, h * half:(h + 1) * half, own] + r2[h, i].astype(jnp.float32)
            acc[i, h * half:(h + 1) * half, own] = total
        for e in range(dests):
            k = c * dests + e
            share = acc[i, e * slots:(e + 1) * slots, own].astype(jnp.bfloat16)

            @pl.when(k < shards - 1)
            def _():
                s3[i, e] = share
                route_copy(i, e, q, k).start()

            @pl.when(k == shards - 1)
            def _():
                arr[q, me] = share

    def step(i, carry):
        @pl.when(i < chunks)
        def _():
            compute(i)

        @pl.when((i >= LAG_SECOND) & (i < chunks + LAG_SECOND))
        def _():
            second(i - LAG_SECOND)

        @pl.when(i >= LAG_ROUTE)
        def _():
            route(i - LAG_ROUTE)

        return carry

    lax.fori_loop(0, chunks + LAG_ROUTE, step, 0)

    def arrive(k, carry):
        source = peer(k)
        for q in range(classes):
            pltpu.make_async_remote_copy(
                src_ref=s3.at[0, 0], dst_ref=arr.at[q, source], send_sem=sem_s3.at[0, 0],
                recv_sem=sem_r3.at[q, source], device_id={"sec": source}, device_id_type=MESH).wait_recv()
        return carry

    lax.fori_loop(0, shards - 1, arrive, 0)

    def place(n, carry):
        for u in range(GROUP):
            slot = n * GROUP + u
            total = None
            for q in range(classes):
                at = recv_sm[q, slot]
                here = arr[q, at // slots, at % slots].astype(jnp.float32)
                total = here if total is None else total + here
            out_ref[slot] = total
        return carry

    lax.fori_loop(0, out_ref.shape[0] // GROUP, place, 0)

    def drain(i, carry):
        for h in range(2):
            first_copy(h, i).wait_send()
            second_copy(h, i).wait_send()
        for e in range(dests):
            k = (i // classes) * dests + e

            @pl.when(k < shards - 1)
            def _():
                route_copy(i, e, i % classes, k).wait_send()
        return carry

    lax.fori_loop(0, chunks, drain, 0)


def routing(target, blocks_here, own_index, shards):
    slots = blocks_here // shards
    slot_ids = jnp.arange(blocks_here, dtype=jnp.int32)
    mine = lax.dynamic_slice_in_dim(target, own_index * blocks_here, blocks_here, 1)
    position = jnp.sum((mine[:, None, :] < mine[:, :, None]).astype(jnp.int32), axis=2)
    send_index = jnp.sum(jnp.where(position[:, None, :] == slot_ids[:, None], slot_ids, 0), axis=2)
    wanted = own_index * blocks_here + slot_ids
    devices = jnp.arange(target.shape[1], dtype=jnp.int32) // blocks_here
    source = jnp.sum(jnp.where(target[:, None, :] == wanted[:, None], devices, 0), axis=2)
    same = (source[:, None, :] == source[:, :, None]) & (slot_ids[None, :] < slot_ids[:, None])
    recv_index = source * slots + jnp.sum(same.astype(jnp.int32), axis=2)
    return send_index, recv_index


def per_device(wavefunction, left_ops, right_ops, left_sector, right_sector, target):
    shards, parts = lax.axis_size("sec"), lax.axis_size("op")
    assert parts == 4
    blocks_here, bl, br = wavefunction.shape
    classes = target.shape[0]
    slots = blocks_here // shards
    chunk = max(slots, GROUP)
    chunks = classes * blocks_here // chunk
    half, rows, dests = chunk // 2, bl // parts, chunk // slots
    send_index, recv_index = routing(target, blocks_here, lax.axis_index("sec"), shards)
    smem, vmem = pl.BlockSpec(memory_space=pltpu.SMEM), pl.BlockSpec(memory_space=pltpu.VMEM)
    wide, narrow = jnp.float32, jnp.bfloat16
    flops = 4 * blocks_here * classes * left_ops.shape[1] * bl * bl * br
    return pl.pallas_call(
        functools.partial(kernel, (shards, classes, chunks, chunk, slots)),
        out_shape=jax.ShapeDtypeStruct((blocks_here, rows, br), wide),
        in_specs=[smem] * 4 + [vmem] * 3,
        out_specs=vmem,
        scratch_shapes=[
            pltpu.VMEM((chunks, chunk, parts, rows, br), wide),
            pltpu.VMEM((2, chunks, half, 2, rows, br), narrow),
            pltpu.VMEM((2, chunks, half, 2, rows, br), narrow),
            pltpu.VMEM((2, chunks, half, rows, br), narrow),
            pltpu.VMEM((2, chunks, half, rows, br), narrow),
            pltpu.VMEM((chunks, dests, slots, rows, br), narrow),
            pltpu.VMEM((classes, shards, slots, rows, br), narrow),
            pltpu.SemaphoreType.DMA((2, chunks)),
            pltpu.SemaphoreType.DMA((2, chunks)),
            pltpu.SemaphoreType.DMA((2, chunks)),
            pltpu.SemaphoreType.DMA((2, chunks)),
            pltpu.SemaphoreType.DMA((chunks, dests)),
            pltpu.SemaphoreType.DMA((classes, shards)),
        ],
        compiler_params=pltpu.CompilerParams(
            collective_id=0, has_side_effects=True, vmem_limit_bytes=48 * 1024 * 1024),
        cost_estimate=pl.CostEstimate(flops=flops, bytes_accessed=8 * 1024 * 1024, transcendentals=0),
    )(left_sector, right_sector, send_index, recv_index, wavefunction, left_ops, right_ops)


def solution(mesh):
    in_specs = (
        P("sec", None, None),
        P(None, "op", None, None, None),
        P(None, "op", None, None, None),
        P("sec"),
        P("sec"),
        P(),
    )
    out_specs = P("sec", "op", None)
    return jax.shard_map(
        per_device, mesh=mesh, in_specs=in_specs, out_specs=out_specs, check_vma=False
    )
```

```python
import functools

import jax
import jax.numpy as jnp
from jax import lax
from jax.experimental import pallas as pl
from jax.experimental.pallas import tpu as pltpu
from jax.sharding import PartitionSpec as P

MESH = pl.DeviceIdType.MESH
GROUP = 8
LAG_SECOND = 2
LAG_ROUTE = 4


def kernel(sizes, left_sm, right_sm, send_sm, recv_sm, w_ref, l_ref, r_ref, out_ref,
           acc, s1, r1, s2, r2, s3, arr, sem_s1, sem_r1, sem_s2, sem_r2, sem_s3, sem_r3):
    shards, classes, chunks, chunk, slots = sizes
    half = chunk // 2
    terms, bl = l_ref.shape[1], l_ref.shape[3]
    rows = acc.shape[3]
    op, me = lax.axis_index("op"), lax.axis_index("sec")
    hi, lo = op // 2, op % 2
    own = hi * 2 + lo
    near_lo, near_hi = hi * 2 + 1 - lo, (1 - hi) * 2 + lo
    dests = chunk // slots

    def peer(k):
        off = shards // 2 + (1 - 2 * (k % 2)) * ((k + 1) // 2)
        return (me + off + shards) % shards

    barrier = pltpu.get_barrier_semaphore()
    for other in (near_lo, near_hi):
        pl.semaphore_signal(barrier, inc=1, device_id={"op": other}, device_id_type=MESH)

    def greet(k, carry):
        pl.semaphore_signal(barrier, inc=1, device_id={"sec": peer(k)}, device_id_type=MESH)
        return carry

    lax.fori_loop(0, shards - 1, greet, 0)
    pl.semaphore_wait(barrier, 2 + shards - 1)

    def first_copy(h, i):
        return pltpu.make_async_remote_copy(
            src_ref=s1.at[h, i], dst_ref=r1.at[h, i], send_sem=sem_s1.at[h, i], recv_sem=sem_r1.at[h, i],
            device_id={"op": near_lo if h == 0 else near_hi}, device_id_type=MESH)

    def second_copy(h, i):
        return pltpu.make_async_remote_copy(
            src_ref=s2.at[h, i], dst_ref=r2.at[h, i], send_sem=sem_s2.at[h, i], recv_sem=sem_r2.at[h, i],
            device_id={"op": near_hi if h == 0 else near_lo}, device_id_type=MESH)

    def route_copy(i, e, q, k):
        return pltpu.make_async_remote_copy(
            src_ref=s3.at[i, e], dst_ref=arr.at[q, me], send_sem=sem_s3.at[i, e], recv_sem=sem_r3.at[q, me],
            device_id={"sec": peer(k)}, device_id_type=MESH)

    def compute(i):
        q, c = i % classes, i // classes
        for b in range(chunk):
            dest = peer(c * dests + b // slots)
            block = send_sm[q, dest * slots + b % slots]
            left = left_sm[block]
            right = right_sm[block]
            mixed = jnp.dot(
                l_ref[q, :, left].reshape(terms * bl, l_ref.shape[4]), w_ref[block],
                preferred_element_type=jnp.float32).astype(jnp.bfloat16)
            mixed = jnp.concatenate([mixed[t * bl:(t + 1) * bl] for t in range(terms)], axis=1)
            rights = jnp.concatenate([r_ref[q, t, right] for t in range(terms)], axis=1)
            value = lax.dot_general(mixed, rights, (((1,), (1,)), ((), ())), preferred_element_type=jnp.float32)
            acc[i, b] = value.reshape(acc.shape[2:])
        for j in range(2):
            s1[0, i, :, j] = acc[i, 0:half, j * 2 + 1 - lo].astype(jnp.bfloat16)
        first_copy(0, i).start()
        for j in range(2):
            s1[1, i, :, j] = acc[i, half:chunk, (1 - hi) * 2 + j].astype(jnp.bfloat16)
        first_copy(1, i).start()

    def second(i):
        first_copy(0, i).wait_recv()
        s2[0, i] = (acc[i, 0:half, near_hi] + r1[0, i, :, 1 - hi].astype(jnp.float32)).astype(jnp.bfloat16)
        second_copy(0, i).start()
        first_copy(1, i).wait_recv()
        s2[1, i] = (acc[i, half:chunk, near_lo] + r1[1, i, :, 1 - lo].astype(jnp.float32)).astype(jnp.bfloat16)
        second_copy(1, i).start()
        acc[i, 0:half, own] = acc[i, 0:half, own] + r1[0, i, :, hi].astype(jnp.float32)
        acc[i, half:chunk, own] = acc[i, half:chunk, own] + r1[1, i, :, lo].astype(jnp.float32)

    def route(i):
        q, c = i % classes, i // classes
        for h in range(2):
            second_copy(h, i).wait_recv()
            total = acc[i, h * half:(h + 1) * half, own] + r2[h, i].astype(jnp.float32)
            acc[i, h * half:(h + 1) * half, own] = total
        for e in range(dests):
            k = c * dests + e
            share = acc[i, e * slots:(e + 1) * slots, own].astype(jnp.bfloat16)

            @pl.when(k < shards - 1)
            def _():
                s3[i, e] = share
                route_copy(i, e, q, k).start()

            @pl.when(k == shards - 1)
            def _():
                arr[q, me] = share

    def step(i, carry):
        @pl.when(i < chunks)
        def _():
            compute(i)

        @pl.when((i >= LAG_SECOND) & (i < chunks + LAG_SECOND))
        def _():
            second(i - LAG_SECOND)

        @pl.when(i >= LAG_ROUTE)
        def _():
            route(i - LAG_ROUTE)

        return carry

    lax.fori_loop(0, chunks + LAG_ROUTE, step, 0)

    def arrive(k, carry):
        source = peer(k)
        for q in range(classes):
            pltpu.make_async_remote_copy(
                src_ref=s3.at[0, 0], dst_ref=arr.at[q, source], send_sem=sem_s3.at[0, 0],
                recv_sem=sem_r3.at[q, source], device_id={"sec": source}, device_id_type=MESH).wait_recv()
        return carry

    lax.fori_loop(0, shards - 1, arrive, 0)

    def place(n, carry):
        for u in range(GROUP):
            slot = n * GROUP + u
            total = None
            for q in range(classes):
                at = recv_sm[q, slot]
                here = arr[q, at // slots, at % slots].astype(jnp.float32)
                total = here if total is None else total + here
            out_ref[slot] = total
        return carry

    lax.fori_loop(0, out_ref.shape[0] // GROUP, place, 0)

    def drain(i, carry):
        for h in range(2):
            first_copy(h, i).wait_send()
            second_copy(h, i).wait_send()
        for e in range(dests):
            k = (i // classes) * dests + e

            @pl.when(k < shards - 1)
            def _():
                route_copy(i, e, i % classes, k).wait_send()
        return carry

    lax.fori_loop(0, chunks, drain, 0)


def routing(target, blocks_here, own_index, shards):
    slots = blocks_here // shards
    slot_ids = jnp.arange(blocks_here, dtype=jnp.int32)
    mine = lax.dynamic_slice_in_dim(target, own_index * blocks_here, blocks_here, 1)
    position = jnp.sum((mine[:, None, :] < mine[:, :, None]).astype(jnp.int32), axis=2)
    send_index = jnp.sum(jnp.where(position[:, None, :] == slot_ids[:, None], slot_ids, 0), axis=2)
    wanted = own_index * blocks_here + slot_ids
    devices = jnp.arange(target.shape[1], dtype=jnp.int32) // blocks_here
    source = jnp.sum(jnp.where(target[:, None, :] == wanted[:, None], devices, 0), axis=2)
    same = (source[:, None, :] == source[:, :, None]) & (slot_ids[None, :] < slot_ids[:, None])
    recv_index = source * slots + jnp.sum(same.astype(jnp.int32), axis=2)
    return send_index, recv_index


def per_device(wavefunction, left_ops, right_ops, left_sector, right_sector, target):
    shards, parts = lax.axis_size("sec"), lax.axis_size("op")
    assert parts == 4
    blocks_here, bl, br = wavefunction.shape
    classes = target.shape[0]
    slots = blocks_here // shards
    chunk = max(slots, GROUP)
    chunks = classes * blocks_here // chunk
    half, rows, dests = chunk // 2, bl // parts, chunk // slots
    send_index, recv_index = routing(target, blocks_here, lax.axis_index("sec"), shards)
    smem, vmem = pl.BlockSpec(memory_space=pltpu.SMEM), pl.BlockSpec(memory_space=pltpu.VMEM)
    wide, narrow = jnp.float32, jnp.bfloat16
    flops = 4 * blocks_here * classes * left_ops.shape[1] * bl * bl * br
    return pl.pallas_call(
        functools.partial(kernel, (shards, classes, chunks, chunk, slots)),
        out_shape=jax.ShapeDtypeStruct((blocks_here, rows, br), wide),
        in_specs=[smem] * 4 + [vmem] * 3,
        out_specs=vmem,
        scratch_shapes=[
            pltpu.VMEM((chunks, chunk, parts, rows, br), wide),
            pltpu.VMEM((2, chunks, half, 2, rows, br), narrow),
            pltpu.VMEM((2, chunks, half, 2, rows, br), narrow),
            pltpu.VMEM((2, chunks, half, rows, br), narrow),
            pltpu.VMEM((2, chunks, half, rows, br), narrow),
            pltpu.VMEM((chunks, dests, slots, rows, br), narrow),
            pltpu.VMEM((classes, shards, slots, rows, br), narrow),
            pltpu.SemaphoreType.DMA((2, chunks)),
            pltpu.SemaphoreType.DMA((2, chunks)),
            pltpu.SemaphoreType.DMA((2, chunks)),
            pltpu.SemaphoreType.DMA((2, chunks)),
            pltpu.SemaphoreType.DMA((chunks, dests)),
            pltpu.SemaphoreType.DMA((classes, shards)),
        ],
        compiler_params=pltpu.CompilerParams(
            collective_id=0, has_side_effects=True, vmem_limit_bytes=48 * 1024 * 1024),
        cost_estimate=pl.CostEstimate(flops=flops, bytes_accessed=8 * 1024 * 1024, transcendentals=0),
    )(left_sector, right_sector, send_index, recv_index, wavefunction, left_ops, right_ops)


def solution(mesh):
    in_specs = (
        P("sec", None, None),
        P(None, "op", None, None, None),
        P(None, "op", None, None, None),
        P("sec"),
        P("sec"),
        P(),
    )
    out_specs = P("sec", "op", None)
    return jax.shard_map(
        per_device, mesh=mesh, in_specs=in_specs, out_specs=out_specs, check_vma=False
    )
```

```python
import functools

import jax
import jax.numpy as jnp
from jax import lax
from jax.experimental import pallas as pl
from jax.experimental.pallas import tpu as pltpu
from jax.sharding import PartitionSpec as P

MESH = pl.DeviceIdType.MESH
GROUP = 8
LAG_SECOND = 2
LAG_ROUTE = 4


def fill_tables(target_ref, table, me, shards, slots):
    classes, total = target_ref.shape
    n = total // shards
    block = lax.broadcasted_iota(jnp.int32, (n, total), 1)
    here = me * n + lax.broadcasted_iota(jnp.int32, (n, total), 0)
    row, col = (lax.broadcasted_iota(jnp.int32, (n, n), axis) for axis in range(2))
    bound = (lax.broadcasted_iota(jnp.int32, (n, shards), 1) + 1) * n

    def count(mask):
        return jnp.sum(jnp.where(mask, 1, 0), axis=1, keepdims=True)

    def as_row(column):
        return jnp.sum(jnp.where(row == col, column, 0), axis=0, keepdims=True)

    for q in range(classes):
        target = target_ref[q:q + 1, :]
        mine = jnp.sum(jnp.where(block == here, target, 0), axis=1, keepdims=True)
        position = count(as_row(mine) < mine)
        order = jnp.sum(jnp.where(position == col, row, 0), axis=0, keepdims=True)
        table[q:q + 1, 0:n] = jnp.minimum(order, n - 1)
        origin = jnp.sum(jnp.where(target == here, block, 0), axis=1, keepdims=True)
        source = count(origin >= bound)
        rank = count((as_row(source) == source) & (col < row))
        table[classes + q:classes + q + 1, 0:n] = jnp.minimum(as_row(source * slots + rank), n - 1)


def kernel(sizes, left_sm, right_sm, target_ref, w_any, l_any, r_any, out_ref,
           w_ref, l_refs, r_refs, table, table_sm, acc, s1, r1, s2, r2, s3, arr,
           sem_in, sem_s1, sem_r1, sem_s2, sem_r2, sem_s3, sem_r3):
    shards, classes, chunks, chunk, slots = sizes
    half = chunk // 2
    terms, bl = l_any.shape[1], l_any.shape[3]
    rows = acc.shape[3]
    op, me = lax.axis_index("op"), lax.axis_index("sec")
    hi, lo = op // 2, op % 2
    own = hi * 2 + lo
    near_lo, near_hi = hi * 2 + 1 - lo, (1 - hi) * 2 + lo
    dests = chunk // slots

    def peer(k):
        off = shards // 2 + (1 - 2 * (k % 2)) * ((k + 1) // 2)
        return (me + off + shards) % shards

    pieces = classes * terms
    part = w_ref.shape[0] // pieces
    for u in range(pieces):
        span = pl.ds(u * part, part)
        pltpu.make_async_copy(w_any.at[span], w_ref.at[span], sem_in.at[2 * classes]).start()
    for q in range(classes):
        for t in range(terms):
            pltpu.make_async_copy(l_any.at[q, t], l_refs[q].at[t], sem_in.at[q]).start()
            pltpu.make_async_copy(r_any.at[q, t], r_refs[q].at[t], sem_in.at[classes + q]).start()

    barrier = pltpu.get_barrier_semaphore()
    for other in (near_lo, near_hi):
        pl.semaphore_signal(barrier, inc=1, device_id={"op": other}, device_id_type=MESH)

    def greet(k, carry):
        pl.semaphore_signal(barrier, inc=1, device_id={"sec": peer(k)}, device_id_type=MESH)
        return carry

    lax.fori_loop(0, shards - 1, greet, 0)
    fill_tables(target_ref, table, me, shards, slots)
    copy = pltpu.make_async_copy(table, table_sm, sem_in.at[2 * classes + 1])
    copy.start()
    copy.wait()
    pltpu.make_async_copy(w_any, w_ref, sem_in.at[2 * classes]).wait()
    pl.semaphore_wait(barrier, 2 + shards - 1)

    def first_copy(h, i):
        return pltpu.make_async_remote_copy(
            src_ref=s1.at[h, i], dst_ref=r1.at[h, i], send_sem=sem_s1.at[h, i], recv_sem=sem_r1.at[h, i],
            device_id={"op": near_lo if h == 0 else near_hi}, device_id_type=MESH)

    def second_copy(h, i):
        return pltpu.make_async_remote_copy(
            src_ref=s2.at[h, i], dst_ref=r2.at[h, i], send_sem=sem_s2.at[h, i], recv_sem=sem_r2.at[h, i],
            device_id={"op": near_hi if h == 0 else near_lo}, device_id_type=MESH)

    def route_copy(i, e, q, k):
        return pltpu.make_async_remote_copy(
            src_ref=s3.at[i, e], dst_ref=arr.at[q, me], send_sem=sem_s3.at[i, e], recv_sem=sem_r3.at[q, me],
            device_id={"sec": peer(k)}, device_id_type=MESH)

    def compute(i, q):
        c = i // classes

        @pl.when(i < classes)
        def _():
            pltpu.make_async_copy(l_any.at[q], l_refs[q], sem_in.at[q]).wait()
            pltpu.make_async_copy(r_any.at[q], r_refs[q], sem_in.at[classes + q]).wait()

        for b in range(chunk):
            dest = peer(c * dests + b // slots)
            block = table_sm[q, dest * slots + b % slots]
            left = left_sm[block]
            right = right_sm[block]
            mixed = jnp.dot(
                l_refs[q][:, left].reshape(terms * bl, l_any.shape[4]), w_ref[block],
                preferred_element_type=jnp.float32).astype(jnp.bfloat16)
            mixed = jnp.concatenate([mixed[t * bl:(t + 1) * bl] for t in range(terms)], axis=1)
            rights = jnp.concatenate([r_refs[q][t, right] for t in range(terms)], axis=1)
            value = lax.dot_general(mixed, rights, (((1,), (1,)), ((), ())), preferred_element_type=jnp.float32)
            acc[i, b] = value.reshape(acc.shape[2:])

    def first(i):
        for j in range(2):
            s1[0, i, :, j] = acc[i, 0:half, j * 2 + 1 - lo].astype(jnp.bfloat16)
        first_copy(0, i).start()
        for j in range(2):
            s1[1, i, :, j] = acc[i, half:chunk, (1 - hi) * 2 + j].astype(jnp.bfloat16)
        first_copy(1, i).start()

    def second(i):
        first_copy(0, i).wait_recv()
        s2[0, i] = (acc[i, 0:half, near_hi] + r1[0, i, :, 1 - hi].astype(jnp.float32)).astype(jnp.bfloat16)
        second_copy(0, i).start()
        first_copy(1, i).wait_recv()
        s2[1, i] = (acc[i, half:chunk, near_lo] + r1[1, i, :, 1 - lo].astype(jnp.float32)).astype(jnp.bfloat16)
        second_copy(1, i).start()
        acc[i, 0:half, own] = acc[i, 0:half, own] + r1[0, i, :, hi].astype(jnp.float32)
        acc[i, half:chunk, own] = acc[i, half:chunk, own] + r1[1, i, :, lo].astype(jnp.float32)

    def route(i):
        q, c = i % classes, i // classes
        for h in range(2):
            second_copy(h, i).wait_recv()
            total = acc[i, h * half:(h + 1) * half, own] + r2[h, i].astype(jnp.float32)
            acc[i, h * half:(h + 1) * half, own] = total
        for e in range(dests):
            k = c * dests + e
            share = acc[i, e * slots:(e + 1) * slots, own].astype(jnp.bfloat16)

            @pl.when(k < shards - 1)
            def _():
                s3[i, e] = share
                route_copy(i, e, q, k).start()

            @pl.when(k == shards - 1)
            def _():
                arr[q, me] = share

    def step(i, carry):
        @pl.when(i < chunks)
        def _():
            for q in range(classes):
                pl.when(i % classes == q)(functools.partial(compute, i, q))
            first(i)

        @pl.when((i >= LAG_SECOND) & (i < chunks + LAG_SECOND))
        def _():
            second(i - LAG_SECOND)

        @pl.when(i >= LAG_ROUTE)
        def _():
            route(i - LAG_ROUTE)

        return carry

    lax.fori_loop(0, chunks + LAG_ROUTE, step, 0)

    def arrive(k, carry):
        source = peer(k)
        for q in range(classes):
            pltpu.make_async_remote_copy(
                src_ref=s3.at[0, 0], dst_ref=arr.at[q, source], send_sem=sem_s3.at[0, 0],
                recv_sem=sem_r3.at[q, source], device_id={"sec": source}, device_id_type=MESH).wait_recv()
        return carry

    lax.fori_loop(0, shards - 1, arrive, 0)

    def place(n, carry):
        for u in range(GROUP):
            slot = n * GROUP + u
            total = None
            for q in range(classes):
                at = table_sm[classes + q, slot]
                here = arr[q, at // slots, at % slots].astype(jnp.float32)
                total = here if total is None else total + here
            out_ref[slot] = total
        return carry

    lax.fori_loop(0, out_ref.shape[0] // GROUP, place, 0)

    def drain(i, carry):
        for h in range(2):
            first_copy(h, i).wait_send()
            second_copy(h, i).wait_send()
        for e in range(dests):
            k = (i // classes) * dests + e

            @pl.when(k < shards - 1)
            def _():
                route_copy(i, e, i % classes, k).wait_send()
        return carry

    lax.fori_loop(0, chunks, drain, 0)


def per_device(wavefunction, left_ops, right_ops, left_sector, right_sector, target):
    shards, parts = lax.axis_size("sec"), lax.axis_size("op")
    assert parts == 4
    blocks_here, bl, br = wavefunction.shape
    classes = target.shape[0]
    slots = blocks_here // shards
    chunk = max(slots, GROUP)
    chunks = classes * blocks_here // chunk
    half, rows, dests = chunk // 2, bl // parts, chunk // slots
    table = (2 * classes + -2 * classes % 8, blocks_here + -blocks_here % 128)
    smem, vmem = pl.BlockSpec(memory_space=pltpu.SMEM), pl.BlockSpec(memory_space=pltpu.VMEM)
    wide, narrow = jnp.float32, jnp.bfloat16
    flops = 4 * blocks_here * classes * left_ops.shape[1] * bl * bl * br
    return pl.pallas_call(
        functools.partial(kernel, (shards, classes, chunks, chunk, slots)),
        out_shape=jax.ShapeDtypeStruct((blocks_here, rows, br), wide),
        in_specs=[smem] * 2 + [vmem] + [pl.BlockSpec(memory_space=pl.ANY)] * 3,
        out_specs=vmem,
        scratch_shapes=[
            pltpu.VMEM(wavefunction.shape, wavefunction.dtype),
            [pltpu.VMEM(left_ops.shape[1:], left_ops.dtype)] * classes,
            [pltpu.VMEM(right_ops.shape[1:], right_ops.dtype)] * classes,
            pltpu.VMEM(table, jnp.int32),
            pltpu.SMEM(table, jnp.int32),
            pltpu.VMEM((chunks, chunk, parts, rows, br), wide),
            pltpu.VMEM((2, chunks, half, 2, rows, br), narrow),
            pltpu.VMEM((2, chunks, half, 2, rows, br), narrow),
            pltpu.VMEM((2, chunks, half, rows, br), narrow),
            pltpu.VMEM((2, chunks, half, rows, br), narrow),
            pltpu.VMEM((chunks, dests, slots, rows, br), narrow),
            pltpu.VMEM((classes, shards, slots, rows, br), narrow),
            pltpu.SemaphoreType.DMA((2 * classes + 2,)),
            pltpu.SemaphoreType.DMA((2, chunks)),
            pltpu.SemaphoreType.DMA((2, chunks)),
            pltpu.SemaphoreType.DMA((2, chunks)),
            pltpu.SemaphoreType.DMA((2, chunks)),
            pltpu.SemaphoreType.DMA((chunks, dests)),
            pltpu.SemaphoreType.DMA((classes, shards)),
        ],
        compiler_params=pltpu.CompilerParams(
            collective_id=0, has_side_effects=True, vmem_limit_bytes=56 * 1024 * 1024),
        cost_estimate=pl.CostEstimate(flops=flops, bytes_accessed=8 * 1024 * 1024, transcendentals=0),
    )(left_sector, right_sector, target, wavefunction, left_ops, right_ops)


def solution(mesh):
    in_specs = (
        P("sec", None, None),
        P(None, "op", None, None, None),
        P(None, "op", None, None, None),
        P("sec"),
        P("sec"),
        P(),
    )
    out_specs = P("sec", "op", None)
    return jax.shard_map(
        per_device, mesh=mesh, in_specs=in_specs, out_specs=out_specs, check_vma=False
    )
```

```python
import functools

import jax
import jax.numpy as jnp
from jax import lax
from jax.experimental import pallas as pl
from jax.experimental.pallas import tpu as pltpu
from jax.sharding import PartitionSpec as P

MESH = pl.DeviceIdType.MESH
GROUP = 4
LAG_SECOND = 4
LAG_ROUTE = 8


def fill_tables(target_ref, table, me, shards, slots):
    classes, total = target_ref.shape
    n = total // shards
    block = lax.broadcasted_iota(jnp.int32, (n, total), 1)
    here = me * n + lax.broadcasted_iota(jnp.int32, (n, total), 0)
    row, col = (lax.broadcasted_iota(jnp.int32, (n, n), axis) for axis in range(2))
    bound = (lax.broadcasted_iota(jnp.int32, (n, shards), 1) + 1) * n

    def count(mask):
        return jnp.sum(jnp.where(mask, 1, 0), axis=1, keepdims=True)

    def as_row(column):
        return jnp.sum(jnp.where(row == col, column, 0), axis=0, keepdims=True)

    for q in range(classes):
        target = target_ref[q:q + 1, :]
        mine = jnp.sum(jnp.where(block == here, target, 0), axis=1, keepdims=True)
        position = count(as_row(mine) < mine)
        order = jnp.sum(jnp.where(position == col, row, 0), axis=0, keepdims=True)
        table[q:q + 1, 0:n] = jnp.minimum(order, n - 1)
        origin = jnp.sum(jnp.where(target == here, block, 0), axis=1, keepdims=True)
        source = count(origin >= bound)
        rank = count((as_row(source) == source) & (col < row))
        table[classes + q:classes + q + 1, 0:n] = jnp.minimum(as_row(source * slots + rank), n - 1)


def kernel(sizes, left_sm, right_sm, target_ref, w_any, l_any, r_any, out_ref,
           w_ref, l_refs, r_refs, table, table_sm, acc, s1, r1, s2, r2, s3, arr,
           sem_in, sem_s1, sem_r1, sem_s2, sem_r2, sem_s3, sem_r3):
    shards, classes, chunks, chunk, slots = sizes
    half = chunk // 2
    terms, bl = l_any.shape[1], l_any.shape[3]
    rows = acc.shape[3]
    op, me = lax.axis_index("op"), lax.axis_index("sec")
    hi, lo = op // 2, op % 2
    own = hi * 2 + lo
    near_lo, near_hi = hi * 2 + 1 - lo, (1 - hi) * 2 + lo
    run = min(chunk, slots)

    def peer(k):
        off = shards // 2 + (1 - 2 * (k % 2)) * ((k + 1) // 2)
        return (me + off + shards) % shards

    pieces = classes * terms
    part = w_ref.shape[0] // pieces
    for u in range(pieces):
        span = pl.ds(u * part, part)
        pltpu.make_async_copy(w_any.at[span], w_ref.at[span], sem_in.at[2 * classes]).start()
    for q in range(classes):
        for t in range(terms):
            pltpu.make_async_copy(l_any.at[q, t], l_refs[q].at[t], sem_in.at[q]).start()
            pltpu.make_async_copy(r_any.at[q, t], r_refs[q].at[t], sem_in.at[classes + q]).start()

    barrier = pltpu.get_barrier_semaphore()
    for other in (near_lo, near_hi):
        pl.semaphore_signal(barrier, inc=1, device_id={"op": other}, device_id_type=MESH)

    def greet(k, carry):
        pl.semaphore_signal(barrier, inc=1, device_id={"sec": peer(k)}, device_id_type=MESH)
        return carry

    lax.fori_loop(0, shards - 1, greet, 0)
    fill_tables(target_ref, table, me, shards, slots)
    copy = pltpu.make_async_copy(table, table_sm, sem_in.at[2 * classes + 1])
    copy.start()
    copy.wait()
    pltpu.make_async_copy(w_any, w_ref, sem_in.at[2 * classes]).wait()
    pl.semaphore_wait(barrier, 2 + shards - 1)

    def first_copy(h, i):
        return pltpu.make_async_remote_copy(
            src_ref=s1.at[h, i], dst_ref=r1.at[h, i], send_sem=sem_s1.at[h, i], recv_sem=sem_r1.at[h, i],
            device_id={"op": near_lo if h == 0 else near_hi}, device_id_type=MESH)

    def second_copy(h, i):
        return pltpu.make_async_remote_copy(
            src_ref=s2.at[h, i], dst_ref=r2.at[h, i], send_sem=sem_s2.at[h, i], recv_sem=sem_r2.at[h, i],
            device_id={"op": near_hi if h == 0 else near_lo}, device_id_type=MESH)

    def route_copy(i, e, q, k, part):
        return pltpu.make_async_remote_copy(
            src_ref=s3.at[i, e], dst_ref=arr.at[q, me, part], send_sem=sem_s3.at[i, e],
            recv_sem=sem_r3.at[q, me, part],
            device_id={"sec": peer(k)}, device_id_type=MESH)

    def compute(i, q):
        c = i // classes

        @pl.when(i < classes)
        def _():
            pltpu.make_async_copy(l_any.at[q], l_refs[q], sem_in.at[q]).wait()
            pltpu.make_async_copy(r_any.at[q], r_refs[q], sem_in.at[classes + q]).wait()

        for b in range(chunk):
            place_at = c * chunk + b
            block = table_sm[q, peer(place_at // slots) * slots + place_at % slots]
            left = left_sm[block]
            right = right_sm[block]
            mixed = jnp.dot(
                l_refs[q][:, left].reshape(terms * bl, l_any.shape[4]), w_ref[block],
                preferred_element_type=jnp.float32).astype(jnp.bfloat16)
            mixed = jnp.concatenate([mixed[t * bl:(t + 1) * bl] for t in range(terms)], axis=1)
            rights = jnp.concatenate([r_refs[q][t, right] for t in range(terms)], axis=1)
            value = lax.dot_general(mixed, rights, (((1,), (1,)), ((), ())), preferred_element_type=jnp.float32)
            acc[i, b] = value.reshape(acc.shape[2:])

    def first(i):
        for j in range(2):
            s1[0, i, :, j] = acc[i, 0:half, j * 2 + 1 - lo].astype(jnp.bfloat16)
        first_copy(0, i).start()
        for j in range(2):
            s1[1, i, :, j] = acc[i, half:chunk, (1 - hi) * 2 + j].astype(jnp.bfloat16)
        first_copy(1, i).start()

    def second(i):
        first_copy(0, i).wait_recv()
        s2[0, i] = (acc[i, 0:half, near_hi] + r1[0, i, :, 1 - hi].astype(jnp.float32)).astype(jnp.bfloat16)
        second_copy(0, i).start()
        first_copy(1, i).wait_recv()
        s2[1, i] = (acc[i, half:chunk, near_lo] + r1[1, i, :, 1 - lo].astype(jnp.float32)).astype(jnp.bfloat16)
        second_copy(1, i).start()
        acc[i, 0:half, own] = acc[i, 0:half, own] + r1[0, i, :, hi].astype(jnp.float32)
        acc[i, half:chunk, own] = acc[i, half:chunk, own] + r1[1, i, :, lo].astype(jnp.float32)

    def route(i):
        q, c = i % classes, i // classes
        for h in range(2):
            second_copy(h, i).wait_recv()
            total = acc[i, h * half:(h + 1) * half, own] + r2[h, i].astype(jnp.float32)
            acc[i, h * half:(h + 1) * half, own] = total
        for e in range(chunk // run):
            at = c * chunk + e * run
            k, part = at // slots, (at % slots) // run
            share = acc[i, e * run:(e + 1) * run, own].astype(jnp.bfloat16)

            @pl.when(k < shards - 1)
            def _():
                s3[i, e] = share
                route_copy(i, e, q, k, part).start()

            @pl.when(k == shards - 1)
            def _():
                arr[q, me, part] = share

    def step(i, carry):
        @pl.when(i < chunks)
        def _():
            for q in range(classes):
                pl.when(i % classes == q)(functools.partial(compute, i, q))
            first(i)

        @pl.when((i >= LAG_SECOND) & (i < chunks + LAG_SECOND))
        def _():
            second(i - LAG_SECOND)

        @pl.when(i >= LAG_ROUTE)
        def _():
            route(i - LAG_ROUTE)

        return carry

    lax.fori_loop(0, chunks + LAG_ROUTE, step, 0)

    def arrive(k, carry):
        source = peer(k)
        for q in range(classes):
            for part in range(slots // run):
                pltpu.make_async_remote_copy(
                    src_ref=s3.at[0, 0], dst_ref=arr.at[q, source, part], send_sem=sem_s3.at[0, 0],
                    recv_sem=sem_r3.at[q, source, part], device_id={"sec": source},
                    device_id_type=MESH).wait_recv()
        return carry

    lax.fori_loop(0, shards - 1, arrive, 0)

    def place(n, carry):
        for u in range(GROUP):
            slot = n * GROUP + u
            total = None
            for q in range(classes):
                at = table_sm[classes + q, slot]
                here = arr[q, at // slots, (at % slots) // run, at % run].astype(jnp.float32)
                total = here if total is None else total + here
            out_ref[slot] = total
        return carry

    lax.fori_loop(0, out_ref.shape[0] // GROUP, place, 0)

    def drain(i, carry):
        for h in range(2):
            first_copy(h, i).wait_send()
            second_copy(h, i).wait_send()
        for e in range(chunk // run):
            at = (i // classes) * chunk + e * run
            k, part = at // slots, (at % slots) // run

            @pl.when(k < shards - 1)
            def _():
                route_copy(i, e, i % classes, k, part).wait_send()
        return carry

    lax.fori_loop(0, chunks, drain, 0)


def per_device(wavefunction, left_ops, right_ops, left_sector, right_sector, target):
    shards, parts = lax.axis_size("sec"), lax.axis_size("op")
    assert parts == 4
    blocks_here, bl, br = wavefunction.shape
    classes = target.shape[0]
    slots = blocks_here // shards
    chunk = min(blocks_here, GROUP)
    chunks = classes * blocks_here // chunk
    run = min(chunk, slots)
    half, rows, dests = chunk // 2, bl // parts, chunk // run
    table = (2 * classes + -2 * classes % 8, blocks_here + -blocks_here % 128)
    smem, vmem = pl.BlockSpec(memory_space=pltpu.SMEM), pl.BlockSpec(memory_space=pltpu.VMEM)
    wide, narrow = jnp.float32, jnp.bfloat16
    flops = 4 * blocks_here * classes * left_ops.shape[1] * bl * bl * br
    return pl.pallas_call(
        functools.partial(kernel, (shards, classes, chunks, chunk, slots)),
        out_shape=jax.ShapeDtypeStruct((blocks_here, rows, br), wide),
        in_specs=[smem] * 2 + [vmem] + [pl.BlockSpec(memory_space=pl.ANY)] * 3,
        out_specs=vmem,
        scratch_shapes=[
            pltpu.VMEM(wavefunction.shape, wavefunction.dtype),
            [pltpu.VMEM(left_ops.shape[1:], left_ops.dtype)] * classes,
            [pltpu.VMEM(right_ops.shape[1:], right_ops.dtype)] * classes,
            pltpu.VMEM(table, jnp.int32),
            pltpu.SMEM(table, jnp.int32),
            pltpu.VMEM((chunks, chunk, parts, rows, br), wide),
            pltpu.VMEM((2, chunks, half, 2, rows, br), narrow),
            pltpu.VMEM((2, chunks, half, 2, rows, br), narrow),
            pltpu.VMEM((2, chunks, half, rows, br), narrow),
            pltpu.VMEM((2, chunks, half, rows, br), narrow),
            pltpu.VMEM((chunks, dests, run, rows, br), narrow),
            pltpu.VMEM((classes, shards, slots // run, run, rows, br), narrow),
            pltpu.SemaphoreType.DMA((2 * classes + 2,)),
            pltpu.SemaphoreType.DMA((2, chunks)),
            pltpu.SemaphoreType.DMA((2, chunks)),
            pltpu.SemaphoreType.DMA((2, chunks)),
            pltpu.SemaphoreType.DMA((2, chunks)),
            pltpu.SemaphoreType.DMA((chunks, dests)),
            pltpu.SemaphoreType.DMA((classes, shards, slots // run)),
        ],
        compiler_params=pltpu.CompilerParams(
            collective_id=0, has_side_effects=True, vmem_limit_bytes=56 * 1024 * 1024),
        cost_estimate=pl.CostEstimate(flops=flops, bytes_accessed=8 * 1024 * 1024, transcendentals=0),
    )(left_sector, right_sector, target, wavefunction, left_ops, right_ops)


def solution(mesh):
    in_specs = (
        P("sec", None, None),
        P(None, "op", None, None, None),
        P(None, "op", None, None, None),
        P("sec"),
        P("sec"),
        P(),
    )
    out_specs = P("sec", "op", None)
    return jax.shard_map(
        per_device, mesh=mesh, in_specs=in_specs, out_specs=out_specs, check_vma=False
    )
```

```python
import functools

import jax
import jax.numpy as jnp
from jax import lax
from jax.experimental import pallas as pl
from jax.experimental.pallas import tpu as pltpu
from jax.sharding import PartitionSpec as P

MESH = pl.DeviceIdType.MESH
GROUP = 8
LAG_SECOND = 2
LAG_ROUTE = 4


def fill_tables(target_ref, table, me, shards, slots):
    classes, total = target_ref.shape
    n = total // shards
    block = lax.broadcasted_iota(jnp.int32, (n, total), 1)
    here = me * n + lax.broadcasted_iota(jnp.int32, (n, total), 0)
    row, col = (lax.broadcasted_iota(jnp.int32, (n, n), axis) for axis in range(2))
    bound = (lax.broadcasted_iota(jnp.int32, (n, shards), 1) + 1) * n

    def count(mask):
        return jnp.sum(jnp.where(mask, 1, 0), axis=1, keepdims=True)

    def as_row(column):
        return jnp.sum(jnp.where(row == col, column, 0), axis=0, keepdims=True)

    for q in range(classes):
        target = target_ref[q:q + 1, :]
        mine = jnp.sum(jnp.where(block == here, target, 0), axis=1, keepdims=True)
        position = count(as_row(mine) < mine)
        order = jnp.sum(jnp.where(position == col, row, 0), axis=0, keepdims=True)
        table[q:q + 1, 0:n] = jnp.minimum(order, n - 1)
        origin = jnp.sum(jnp.where(target == here, block, 0), axis=1, keepdims=True)
        source = count(origin >= bound)
        rank = count((as_row(source) == source) & (col < row))
        table[classes + q:classes + q + 1, 0:n] = jnp.minimum(as_row(source * slots + rank), n - 1)


def kernel(sizes, left_sm, right_sm, target_ref, w_any, l_any, r_any, out_ref,
           w_ref, l_refs, r_refs, table, table_sm, acc, s1, r1, s2, r2, s3, arr,
           sem_in, sem_s1, sem_r1, sem_s2, sem_r2, sem_s3, sem_r3):
    shards, classes, chunks, chunk, slots = sizes
    half = chunk // 2
    terms, bl = l_any.shape[1], l_any.shape[3]
    rows = acc.shape[3]
    op, me = lax.axis_index("op"), lax.axis_index("sec")
    hi, lo = op // 2, op % 2
    own = hi * 2 + lo
    near_lo, near_hi = hi * 2 + 1 - lo, (1 - hi) * 2 + lo
    run = min(chunk, slots)

    def peer(k):
        off = shards // 2 + (1 - 2 * (k % 2)) * ((k + 1) // 2)
        return (me + off + shards) % shards

    pieces = classes * terms
    part = w_ref.shape[0] // pieces
    for u in range(pieces):
        span = pl.ds(u * part, part)
        pltpu.make_async_copy(w_any.at[span], w_ref.at[span], sem_in.at[2 * classes]).start()
    for q in range(classes):
        for t in range(terms):
            pltpu.make_async_copy(l_any.at[q, t], l_refs[q].at[t], sem_in.at[q]).start()
            pltpu.make_async_copy(r_any.at[q, t], r_refs[q].at[t], sem_in.at[classes + q]).start()

    barrier = pltpu.get_barrier_semaphore()
    for other in (near_lo, near_hi):
        pl.semaphore_signal(barrier, inc=1, device_id={"op": other}, device_id_type=MESH)

    def greet(k, carry):
        pl.semaphore_signal(barrier, inc=1, device_id={"sec": peer(k)}, device_id_type=MESH)
        return carry

    lax.fori_loop(0, shards - 1, greet, 0)
    fill_tables(target_ref, table, me, shards, slots)
    copy = pltpu.make_async_copy(table, table_sm, sem_in.at[2 * classes + 1])
    copy.start()
    copy.wait()
    pltpu.make_async_copy(w_any, w_ref, sem_in.at[2 * classes]).wait()
    pl.semaphore_wait(barrier, 2 + shards - 1)

    def first_copy(h, i):
        return pltpu.make_async_remote_copy(
            src_ref=s1.at[h, i], dst_ref=r1.at[h, i], send_sem=sem_s1.at[h, i], recv_sem=sem_r1.at[h, i],
            device_id={"op": near_lo if h == 0 else near_hi}, device_id_type=MESH)

    def second_copy(h, i):
        return pltpu.make_async_remote_copy(
            src_ref=s2.at[h, i], dst_ref=r2.at[h, i], send_sem=sem_s2.at[h, i], recv_sem=sem_r2.at[h, i],
            device_id={"op": near_hi if h == 0 else near_lo}, device_id_type=MESH)

    def route_copy(i, e, q, k, part):
        return pltpu.make_async_remote_copy(
            src_ref=s3.at[i, e], dst_ref=arr.at[q, me, part], send_sem=sem_s3.at[i, e],
            recv_sem=sem_r3.at[q, me, part],
            device_id={"sec": peer(k)}, device_id_type=MESH)

    def compute(i, q):
        c = i // classes

        @pl.when(i < classes)
        def _():
            pltpu.make_async_copy(l_any.at[q], l_refs[q], sem_in.at[q]).wait()
            pltpu.make_async_copy(r_any.at[q], r_refs[q], sem_in.at[classes + q]).wait()

            def turn(sector, carry):
                for t in range(terms):
                    r_refs[q][t, sector] = r_refs[q][t, sector].T
                return carry

            lax.fori_loop(0, r_any.shape[2], turn, 0)

        for b in range(chunk):
            place_at = c * chunk + b
            block = table_sm[q, peer(place_at // slots) * slots + place_at % slots]
            left = left_sm[block]
            right = right_sm[block]
            mixed = jnp.dot(
                l_refs[q][:, left].reshape(terms * bl, l_any.shape[4]), w_ref[block],
                preferred_element_type=jnp.float32).astype(jnp.bfloat16)
            mixed = jnp.concatenate([mixed[t * bl:(t + 1) * bl] for t in range(terms)], axis=1)
            rights = r_refs[q][:, right].reshape(terms * r_any.shape[4], r_any.shape[3])
            value = jnp.dot(mixed, rights, preferred_element_type=jnp.float32)
            acc[i, b] = value.reshape(acc.shape[2:])

    def first(i):
        for j in range(2):
            s1[0, i, :, j] = acc[i, 0:half, j * 2 + 1 - lo].astype(jnp.bfloat16)
        first_copy(0, i).start()
        for j in range(2):
            s1[1, i, :, j] = acc[i, half:chunk, (1 - hi) * 2 + j].astype(jnp.bfloat16)
        first_copy(1, i).start()

    def second(i):
        first_copy(0, i).wait_recv()
        s2[0, i] = (acc[i, 0:half, near_hi] + r1[0, i, :, 1 - hi].astype(jnp.float32)).astype(jnp.bfloat16)
        second_copy(0, i).start()
        first_copy(1, i).wait_recv()
        s2[1, i] = (acc[i, half:chunk, near_lo] + r1[1, i, :, 1 - lo].astype(jnp.float32)).astype(jnp.bfloat16)
        second_copy(1, i).start()
        acc[i, 0:half, own] = acc[i, 0:half, own] + r1[0, i, :, hi].astype(jnp.float32)
        acc[i, half:chunk, own] = acc[i, half:chunk, own] + r1[1, i, :, lo].astype(jnp.float32)

    def route(i):
        q, c = i % classes, i // classes
        for h in range(2):
            second_copy(h, i).wait_recv()
            total = acc[i, h * half:(h + 1) * half, own] + r2[h, i].astype(jnp.float32)
            acc[i, h * half:(h + 1) * half, own] = total
        for e in range(chunk // run):
            at = c * chunk + e * run
            k, part = at // slots, (at % slots) // run
            share = acc[i, e * run:(e + 1) * run, own].astype(jnp.bfloat16)

            @pl.when(k < shards - 1)
            def _():
                s3[i, e] = share
                route_copy(i, e, q, k, part).start()

            @pl.when(k == shards - 1)
            def _():
                arr[q, me, part] = share

    def step(i, carry):
        @pl.when(i < chunks)
        def _():
            for q in range(classes):
                pl.when(i % classes == q)(functools.partial(compute, i, q))
            first(i)

        @pl.when((i >= LAG_SECOND) & (i < chunks + LAG_SECOND))
        def _():
            second(i - LAG_SECOND)

        @pl.when(i >= LAG_ROUTE)
        def _():
            route(i - LAG_ROUTE)

        return carry

    lax.fori_loop(0, chunks + LAG_ROUTE, step, 0)

    def arrive(k, carry):
        source = peer(k)
        for q in range(classes):
            for part in range(slots // run):
                pltpu.make_async_remote_copy(
                    src_ref=s3.at[0, 0], dst_ref=arr.at[q, source, part], send_sem=sem_s3.at[0, 0],
                    recv_sem=sem_r3.at[q, source, part], device_id={"sec": source},
                    device_id_type=MESH).wait_recv()
        return carry

    lax.fori_loop(0, shards - 1, arrive, 0)

    def place(n, carry):
        for u in range(GROUP):
            slot = n * GROUP + u
            total = None
            for q in range(classes):
                at = table_sm[classes + q, slot]
                here = arr[q, at // slots, (at % slots) // run, at % run].astype(jnp.float32)
                total = here if total is None else total + here
            out_ref[slot] = total
        return carry

    lax.fori_loop(0, out_ref.shape[0] // GROUP, place, 0)

    def drain(i, carry):
        for h in range(2):
            first_copy(h, i).wait_send()
            second_copy(h, i).wait_send()
        for e in range(chunk // run):
            at = (i // classes) * chunk + e * run
            k, part = at // slots, (at % slots) // run

            @pl.when(k < shards - 1)
            def _():
                route_copy(i, e, i % classes, k, part).wait_send()
        return carry

    lax.fori_loop(0, chunks, drain, 0)


def per_device(wavefunction, left_ops, right_ops, left_sector, right_sector, target):
    shards, parts = lax.axis_size("sec"), lax.axis_size("op")
    assert parts == 4
    blocks_here, bl, br = wavefunction.shape
    classes = target.shape[0]
    slots = blocks_here // shards
    chunk = min(blocks_here, GROUP)
    chunks = classes * blocks_here // chunk
    run = min(chunk, slots)
    half, rows, dests = chunk // 2, bl // parts, chunk // run
    table = (2 * classes + -2 * classes % 8, blocks_here + -blocks_here % 128)
    smem, vmem = pl.BlockSpec(memory_space=pltpu.SMEM), pl.BlockSpec(memory_space=pltpu.VMEM)
    wide, narrow = jnp.float32, jnp.bfloat16
    flops = 4 * blocks_here * classes * left_ops.shape[1] * bl * bl * br
    return pl.pallas_call(
        functools.partial(kernel, (shards, classes, chunks, chunk, slots)),
        out_shape=jax.ShapeDtypeStruct((blocks_here, rows, br), wide),
        in_specs=[smem] * 2 + [vmem] + [pl.BlockSpec(memory_space=pl.ANY)] * 3,
        out_specs=vmem,
        scratch_shapes=[
            pltpu.VMEM(wavefunction.shape, wavefunction.dtype),
            [pltpu.VMEM(left_ops.shape[1:], left_ops.dtype)] * classes,
            [pltpu.VMEM(right_ops.shape[1:], right_ops.dtype)] * classes,
            pltpu.VMEM(table, jnp.int32),
            pltpu.SMEM(table, jnp.int32),
            pltpu.VMEM((chunks, chunk, parts, rows, br), wide),
            pltpu.VMEM((2, chunks, half, 2, rows, br), narrow),
            pltpu.VMEM((2, chunks, half, 2, rows, br), narrow),
            pltpu.VMEM((2, chunks, half, rows, br), narrow),
            pltpu.VMEM((2, chunks, half, rows, br), narrow),
            pltpu.VMEM((chunks, dests, run, rows, br), narrow),
            pltpu.VMEM((classes, shards, slots // run, run, rows, br), narrow),
            pltpu.SemaphoreType.DMA((2 * classes + 2,)),
            pltpu.SemaphoreType.DMA((2, chunks)),
            pltpu.SemaphoreType.DMA((2, chunks)),
            pltpu.SemaphoreType.DMA((2, chunks)),
            pltpu.SemaphoreType.DMA((2, chunks)),
            pltpu.SemaphoreType.DMA((chunks, dests)),
            pltpu.SemaphoreType.DMA((classes, shards, slots // run)),
        ],
        compiler_params=pltpu.CompilerParams(
            collective_id=0, has_side_effects=True, vmem_limit_bytes=56 * 1024 * 1024),
        cost_estimate=pl.CostEstimate(flops=flops, bytes_accessed=8 * 1024 * 1024, transcendentals=0),
    )(left_sector, right_sector, target, wavefunction, left_ops, right_ops)


def solution(mesh):
    in_specs = (
        P("sec", None, None),
        P(None, "op", None, None, None),
        P(None, "op", None, None, None),
        P("sec"),
        P("sec"),
        P(),
    )
    out_specs = P("sec", "op", None)
    return jax.shard_map(
        per_device, mesh=mesh, in_specs=in_specs, out_specs=out_specs, check_vma=False
    )
```

```python
import functools

import jax
import jax.numpy as jnp
from jax import lax
from jax.experimental import pallas as pl
from jax.experimental.pallas import tpu as pltpu
from jax.sharding import PartitionSpec as P

MESH = pl.DeviceIdType.MESH
GROUP = 8
LAG_SECOND = 3
LAG_ROUTE = 6


def fill_tables(target_ref, table, me, shards, slots):
    classes, total = target_ref.shape
    n = total // shards
    block = lax.broadcasted_iota(jnp.int32, (n, total), 1)
    here = me * n + lax.broadcasted_iota(jnp.int32, (n, total), 0)
    row, col = (lax.broadcasted_iota(jnp.int32, (n, n), axis) for axis in range(2))
    bound = (lax.broadcasted_iota(jnp.int32, (n, shards), 1) + 1) * n

    def count(mask):
        return jnp.sum(jnp.where(mask, 1, 0), axis=1, keepdims=True)

    def as_row(column):
        return jnp.sum(jnp.where(row == col, column, 0), axis=0, keepdims=True)

    for q in range(classes):
        target = target_ref[q:q + 1, :]
        mine = jnp.sum(jnp.where(block == here, target, 0), axis=1, keepdims=True)
        position = count(as_row(mine) < mine)
        order = jnp.sum(jnp.where(position == col, row, 0), axis=0, keepdims=True)
        table[q:q + 1, 0:n] = jnp.minimum(order, n - 1)
        origin = jnp.sum(jnp.where(target == here, block, 0), axis=1, keepdims=True)
        source = count(origin >= bound)
        rank = count((as_row(source) == source) & (col < row))
        table[classes + q:classes + q + 1, 0:n] = jnp.minimum(as_row(source * slots + rank), n - 1)


def kernel(sizes, left_sm, right_sm, target_ref, w_any, l_any, r_any, out_ref,
           w_ref, l_refs, r_refs, table, table_sm, acc, s1, r1, s2, r2, s3, arr,
           sem_in, sem_s1, sem_r1, sem_s2, sem_r2, sem_s3, sem_r3):
    shards, classes, chunks, chunk, slots = sizes
    half = chunk // 2
    terms, bl = l_any.shape[1], l_any.shape[3]
    rows = acc.shape[3]
    op, me = lax.axis_index("op"), lax.axis_index("sec")
    hi, lo = op // 2, op % 2
    own = hi * 2 + lo
    near_lo, near_hi = hi * 2 + 1 - lo, (1 - hi) * 2 + lo
    run = min(chunk, slots)

    def peer(k):
        off = shards // 2 + (1 - 2 * (k % 2)) * ((k + 1) // 2)
        return (me + off + shards) % shards

    pieces = classes * terms
    part = w_ref.shape[0] // pieces
    for u in range(pieces):
        span = pl.ds(u * part, part)
        pltpu.make_async_copy(w_any.at[span], w_ref.at[span], sem_in.at[2 * classes]).start()
    for q in range(classes):
        for t in range(terms):
            pltpu.make_async_copy(l_any.at[q, t], l_refs[q].at[t], sem_in.at[q]).start()
            pltpu.make_async_copy(r_any.at[q, t], r_refs[q].at[t], sem_in.at[classes + q]).start()

    barrier = pltpu.get_barrier_semaphore()
    for other in (near_lo, near_hi):
        pl.semaphore_signal(barrier, inc=1, device_id={"op": other}, device_id_type=MESH)

    def greet(k, carry):
        pl.semaphore_signal(barrier, inc=1, device_id={"sec": peer(k)}, device_id_type=MESH)
        return carry

    lax.fori_loop(0, shards - 1, greet, 0)
    fill_tables(target_ref, table, me, shards, slots)
    copy = pltpu.make_async_copy(table, table_sm, sem_in.at[2 * classes + 1])
    copy.start()
    copy.wait()
    pltpu.make_async_copy(w_any, w_ref, sem_in.at[2 * classes]).wait()
    def first_copy(h, i):
        return pltpu.make_async_remote_copy(
            src_ref=s1.at[h, i], dst_ref=r1.at[h, i], send_sem=sem_s1.at[h, i], recv_sem=sem_r1.at[h, i],
            device_id={"op": near_lo if h == 0 else near_hi}, device_id_type=MESH)

    def second_copy(h, i):
        return pltpu.make_async_remote_copy(
            src_ref=s2.at[h, i], dst_ref=r2.at[h, i], send_sem=sem_s2.at[h, i], recv_sem=sem_r2.at[h, i],
            device_id={"op": near_hi if h == 0 else near_lo}, device_id_type=MESH)

    def route_copy(i, e, q, k, part):
        return pltpu.make_async_remote_copy(
            src_ref=s3.at[i, e], dst_ref=arr.at[q, me, part], send_sem=sem_s3.at[i, e],
            recv_sem=sem_r3.at[q, me, part],
            device_id={"sec": peer(k)}, device_id_type=MESH)

    def compute(i, q):
        c = i // classes

        @pl.when(jnp.int32(i) < classes)
        def _():
            pltpu.make_async_copy(l_any.at[q], l_refs[q], sem_in.at[q]).wait()
            pltpu.make_async_copy(r_any.at[q], r_refs[q], sem_in.at[classes + q]).wait()

        for b in range(chunk):
            place_at = c * chunk + b
            block = table_sm[q, peer(place_at // slots) * slots + place_at % slots]
            left = left_sm[block]
            right = right_sm[block]
            mixed = jnp.dot(
                l_refs[q][:, left].reshape(terms * bl, l_any.shape[4]), w_ref[block],
                preferred_element_type=jnp.float32).astype(jnp.bfloat16)
            mixed = jnp.concatenate([mixed[t * bl:(t + 1) * bl] for t in range(terms)], axis=1)
            rights = jnp.concatenate([r_refs[q][t, right] for t in range(terms)], axis=1)
            value = lax.dot_general(mixed, rights, (((1,), (1,)), ((), ())), preferred_element_type=jnp.float32)
            acc[i, b] = value.reshape(acc.shape[2:])

    def first(i):
        for j in range(2):
            s1[0, i, :, j] = acc[i, 0:half, j * 2 + 1 - lo].astype(jnp.bfloat16)
        first_copy(0, i).start()
        for j in range(2):
            s1[1, i, :, j] = acc[i, half:chunk, (1 - hi) * 2 + j].astype(jnp.bfloat16)
        first_copy(1, i).start()

    def second(i):
        first_copy(0, i).wait_recv()
        s2[0, i] = (acc[i, 0:half, near_hi] + r1[0, i, :, 1 - hi].astype(jnp.float32)).astype(jnp.bfloat16)
        second_copy(0, i).start()
        first_copy(1, i).wait_recv()
        s2[1, i] = (acc[i, half:chunk, near_lo] + r1[1, i, :, 1 - lo].astype(jnp.float32)).astype(jnp.bfloat16)
        second_copy(1, i).start()
        acc[i, 0:half, own] = acc[i, 0:half, own] + r1[0, i, :, hi].astype(jnp.float32)
        acc[i, half:chunk, own] = acc[i, half:chunk, own] + r1[1, i, :, lo].astype(jnp.float32)

    def route(i):
        q, c = i % classes, i // classes
        for h in range(2):
            second_copy(h, i).wait_recv()
            total = acc[i, h * half:(h + 1) * half, own] + r2[h, i].astype(jnp.float32)
            acc[i, h * half:(h + 1) * half, own] = total
        for e in range(chunk // run):
            at = c * chunk + e * run
            k, part = at // slots, (at % slots) // run
            share = acc[i, e * run:(e + 1) * run, own].astype(jnp.bfloat16)

            @pl.when(k < shards - 1)
            def _():
                s3[i, e] = share
                route_copy(i, e, q, k, part).start()

            @pl.when(k == shards - 1)
            def _():
                arr[q, me, part] = share

    def step(i, carry):
        @pl.when(i < chunks)
        def _():
            for q in range(classes):
                pl.when((i % classes == q) & (i > 0))(functools.partial(compute, i, q))
            first(i)

        @pl.when((i >= LAG_SECOND) & (i < chunks + LAG_SECOND))
        def _():
            second(i - LAG_SECOND)

        @pl.when(i >= LAG_ROUTE)
        def _():
            route(i - LAG_ROUTE)

        return carry

    compute(0, 0)
    pl.semaphore_wait(barrier, 2 + shards - 1)
    lax.fori_loop(0, chunks + LAG_ROUTE, step, 0)

    def arrive(k, carry):
        source = peer(k)
        for q in range(classes):
            for part in range(slots // run):
                pltpu.make_async_remote_copy(
                    src_ref=s3.at[0, 0], dst_ref=arr.at[q, source, part], send_sem=sem_s3.at[0, 0],
                    recv_sem=sem_r3.at[q, source, part], device_id={"sec": source},
                    device_id_type=MESH).wait_recv()
        return carry

    lax.fori_loop(0, shards - 1, arrive, 0)

    def place(n, carry):
        for u in range(GROUP):
            slot = n * GROUP + u
            total = None
            for q in range(classes):
                at = table_sm[classes + q, slot]
                here = arr[q, at // slots, (at % slots) // run, at % run].astype(jnp.float32)
                total = here if total is None else total + here
            out_ref[slot] = total
        return carry

    lax.fori_loop(0, out_ref.shape[0] // GROUP, place, 0)

    def drain(i, carry):
        for h in range(2):
            first_copy(h, i).wait_send()
            second_copy(h, i).wait_send()
        for e in range(chunk // run):
            at = (i // classes) * chunk + e * run
            k, part = at // slots, (at % slots) // run

            @pl.when(k < shards - 1)
            def _():
                route_copy(i, e, i % classes, k, part).wait_send()
        return carry

    lax.fori_loop(0, chunks, drain, 0)


def per_device(wavefunction, left_ops, right_ops, left_sector, right_sector, target):
    shards, parts = lax.axis_size("sec"), lax.axis_size("op")
    assert parts == 4
    blocks_here, bl, br = wavefunction.shape
    classes = target.shape[0]
    slots = blocks_here // shards
    chunk = min(blocks_here, GROUP)
    chunks = classes * blocks_here // chunk
    run = min(chunk, slots)
    half, rows, dests = chunk // 2, bl // parts, chunk // run
    table = (2 * classes + -2 * classes % 8, blocks_here + -blocks_here % 128)
    smem, vmem = pl.BlockSpec(memory_space=pltpu.SMEM), pl.BlockSpec(memory_space=pltpu.VMEM)
    wide, narrow = jnp.float32, jnp.bfloat16
    flops = 4 * blocks_here * classes * left_ops.shape[1] * bl * bl * br
    return pl.pallas_call(
        functools.partial(kernel, (shards, classes, chunks, chunk, slots)),
        out_shape=jax.ShapeDtypeStruct((blocks_here, rows, br), wide),
        in_specs=[smem] * 2 + [vmem] + [pl.BlockSpec(memory_space=pl.ANY)] * 3,
        out_specs=vmem,
        scratch_shapes=[
            pltpu.VMEM(wavefunction.shape, wavefunction.dtype),
            [pltpu.VMEM(left_ops.shape[1:], left_ops.dtype)] * classes,
            [pltpu.VMEM(right_ops.shape[1:], right_ops.dtype)] * classes,
            pltpu.VMEM(table, jnp.int32),
            pltpu.SMEM(table, jnp.int32),
            pltpu.VMEM((chunks, chunk, parts, rows, br), wide),
            pltpu.VMEM((2, chunks, half, 2, rows, br), narrow),
            pltpu.VMEM((2, chunks, half, 2, rows, br), narrow),
            pltpu.VMEM((2, chunks, half, rows, br), narrow),
            pltpu.VMEM((2, chunks, half, rows, br), narrow),
            pltpu.VMEM((chunks, dests, run, rows, br), narrow),
            pltpu.VMEM((classes, shards, slots // run, run, rows, br), narrow),
            pltpu.SemaphoreType.DMA((2 * classes + 2,)),
            pltpu.SemaphoreType.DMA((2, chunks)),
            pltpu.SemaphoreType.DMA((2, chunks)),
            pltpu.SemaphoreType.DMA((2, chunks)),
            pltpu.SemaphoreType.DMA((2, chunks)),
            pltpu.SemaphoreType.DMA((chunks, dests)),
            pltpu.SemaphoreType.DMA((classes, shards, slots // run)),
        ],
        compiler_params=pltpu.CompilerParams(
            collective_id=0, has_side_effects=True, vmem_limit_bytes=56 * 1024 * 1024),
        cost_estimate=pl.CostEstimate(flops=flops, bytes_accessed=8 * 1024 * 1024, transcendentals=0),
    )(left_sector, right_sector, target, wavefunction, left_ops, right_ops)


def solution(mesh):
    in_specs = (
        P("sec", None, None),
        P(None, "op", None, None, None),
        P(None, "op", None, None, None),
        P("sec"),
        P("sec"),
        P(),
    )
    out_specs = P("sec", "op", None)
    return jax.shard_map(
        per_device, mesh=mesh, in_specs=in_specs, out_specs=out_specs, check_vma=False
    )
```

```python
import functools

import jax
import jax.numpy as jnp
from jax import lax
from jax.experimental import pallas as pl
from jax.experimental.pallas import tpu as pltpu
from jax.sharding import PartitionSpec as P

MESH = pl.DeviceIdType.MESH
GROUP = 8
BESIDE = 4
LAG_SECOND = 3
LAG_ROUTE = 6


def fill_tables(target_ref, table, me, shards, slots):
    classes, total = target_ref.shape
    n = total // shards
    block = lax.broadcasted_iota(jnp.int32, (n, total), 1)
    here = me * n + lax.broadcasted_iota(jnp.int32, (n, total), 0)
    row, col = (lax.broadcasted_iota(jnp.int32, (n, n), axis) for axis in range(2))
    bound = (lax.broadcasted_iota(jnp.int32, (n, shards), 1) + 1) * n

    def count(mask):
        return jnp.sum(jnp.where(mask, 1, 0), axis=1, keepdims=True)

    def as_row(column):
        return jnp.sum(jnp.where(row == col, column, 0), axis=0, keepdims=True)

    for q in range(classes):
        target = target_ref[q:q + 1, :]
        mine = jnp.sum(jnp.where(block == here, target, 0), axis=1, keepdims=True)
        position = count(as_row(mine) < mine)
        order = jnp.sum(jnp.where(position == col, row, 0), axis=0, keepdims=True)
        table[q:q + 1, 0:n] = jnp.minimum(order, n - 1)
        origin = jnp.sum(jnp.where(target == here, block, 0), axis=1, keepdims=True)
        source = count(origin >= bound)
        rank = count((as_row(source) == source) & (col < row))
        table[classes + q:classes + q + 1, 0:n] = jnp.minimum(as_row(source * slots + rank), n - 1)


def kernel(sizes, left_sm, right_sm, target_ref, w_any, l_any, r_any, out_ref,
           w_ref, l_refs, r_refs, table, table_sm, acc, s1, r1, s2, r2, s3, arr,
           sem_in, sem_s1, sem_r1, sem_s2, sem_r2, sem_s3, sem_r3):
    shards, classes, chunks, chunk, slots = sizes
    half = chunk // 2
    terms, bl = l_any.shape[1], l_any.shape[3]
    rows = acc.shape[3]
    op, me = lax.axis_index("op"), lax.axis_index("sec")
    hi, lo = op // 2, op % 2
    own = hi * 2 + lo
    near_lo, near_hi = hi * 2 + 1 - lo, (1 - hi) * 2 + lo
    run = min(chunk, slots)

    def peer(k):
        off = shards // 2 + (1 - 2 * (k % 2)) * ((k + 1) // 2)
        return (me + off + shards) % shards

    pieces = classes * terms
    part = w_ref.shape[0] // pieces
    for u in range(pieces):
        span = pl.ds(u * part, part)
        pltpu.make_async_copy(w_any.at[span], w_ref.at[span], sem_in.at[2 * classes]).start()
    for q in range(classes):
        for t in range(terms):
            pltpu.make_async_copy(l_any.at[q, t], l_refs[q].at[t], sem_in.at[q]).start()
            pltpu.make_async_copy(r_any.at[q, t], r_refs[q].at[t], sem_in.at[classes + q]).start()

    barrier = pltpu.get_barrier_semaphore()
    for other in (near_lo, near_hi):
        pl.semaphore_signal(barrier, inc=1, device_id={"op": other}, device_id_type=MESH)

    def greet(k, carry):
        pl.semaphore_signal(barrier, inc=1, device_id={"sec": peer(k)}, device_id_type=MESH)
        return carry

    lax.fori_loop(0, shards - 1, greet, 0)
    fill_tables(target_ref, table, me, shards, slots)
    copy = pltpu.make_async_copy(table, table_sm, sem_in.at[2 * classes + 1])
    copy.start()
    copy.wait()
    pltpu.make_async_copy(w_any, w_ref, sem_in.at[2 * classes]).wait()
    def first_copy(h, i):
        return pltpu.make_async_remote_copy(
            src_ref=s1.at[h, i], dst_ref=r1.at[h, i], send_sem=sem_s1.at[h, i], recv_sem=sem_r1.at[h, i],
            device_id={"op": near_lo if h == 0 else near_hi}, device_id_type=MESH)

    def second_copy(h, i):
        return pltpu.make_async_remote_copy(
            src_ref=s2.at[h, i], dst_ref=r2.at[h, i], send_sem=sem_s2.at[h, i], recv_sem=sem_r2.at[h, i],
            device_id={"op": near_hi if h == 0 else near_lo}, device_id_type=MESH)

    def route_copy(i, e, q, k, part):
        return pltpu.make_async_remote_copy(
            src_ref=s3.at[i, e], dst_ref=arr.at[q, me, part], send_sem=sem_s3.at[i, e],
            recv_sem=sem_r3.at[q, me, part],
            device_id={"sec": peer(k)}, device_id_type=MESH)

    def compute(i, q):
        c = i // classes

        @pl.when(jnp.int32(i) < classes)
        def _():
            pltpu.make_async_copy(l_any.at[q], l_refs[q], sem_in.at[q]).wait()
            pltpu.make_async_copy(r_any.at[q], r_refs[q], sem_in.at[classes + q]).wait()

        for start in range(0, chunk, BESIDE):
            spots = []
            for b in range(start, min(start + BESIDE, chunk)):
                place_at = c * chunk + b
                block = table_sm[q, peer(place_at // slots) * slots + place_at % slots]
                spots.append((b, block, left_sm[block], right_sm[block]))
            mixes = []
            for b, block, left, right in spots:
                mixed = jnp.dot(
                    l_refs[q][:, left].reshape(terms * bl, l_any.shape[4]), w_ref[block],
                    preferred_element_type=jnp.float32).astype(jnp.bfloat16)
                mixes.append(jnp.concatenate([mixed[t * bl:(t + 1) * bl] for t in range(terms)], axis=1))
            values = []
            for (b, block, left, right), mixed in zip(spots, mixes):
                rights = jnp.concatenate([r_refs[q][t, right] for t in range(terms)], axis=1)
                values.append(lax.dot_general(
                    mixed, rights, (((1,), (1,)), ((), ())), preferred_element_type=jnp.float32))
            for (b, block, left, right), value in zip(spots, values):
                acc[i, b] = value.reshape(acc.shape[2:])

    def first(i):
        for j in range(2):
            s1[0, i, :, j] = acc[i, 0:half, j * 2 + 1 - lo].astype(jnp.bfloat16)
        first_copy(0, i).start()
        for j in range(2):
            s1[1, i, :, j] = acc[i, half:chunk, (1 - hi) * 2 + j].astype(jnp.bfloat16)
        first_copy(1, i).start()

    def second(i):
        first_copy(0, i).wait_recv()
        s2[0, i] = (acc[i, 0:half, near_hi] + r1[0, i, :, 1 - hi].astype(jnp.float32)).astype(jnp.bfloat16)
        second_copy(0, i).start()
        first_copy(1, i).wait_recv()
        s2[1, i] = (acc[i, half:chunk, near_lo] + r1[1, i, :, 1 - lo].astype(jnp.float32)).astype(jnp.bfloat16)
        second_copy(1, i).start()
        acc[i, 0:half, own] = acc[i, 0:half, own] + r1[0, i, :, hi].astype(jnp.float32)
        acc[i, half:chunk, own] = acc[i, half:chunk, own] + r1[1, i, :, lo].astype(jnp.float32)

    def route(i):
        q, c = i % classes, i // classes
        for h in range(2):
            second_copy(h, i).wait_recv()
            total = acc[i, h * half:(h + 1) * half, own] + r2[h, i].astype(jnp.float32)
            acc[i, h * half:(h + 1) * half, own] = total
        for e in range(chunk // run):
            at = c * chunk + e * run
            k, part = at // slots, (at % slots) // run
            share = acc[i, e * run:(e + 1) * run, own].astype(jnp.bfloat16)

            @pl.when(k < shards - 1)
            def _():
                s3[i, e] = share
                route_copy(i, e, q, k, part).start()

            @pl.when(k == shards - 1)
            def _():
                arr[q, me, part] = share

    def step(i, carry):
        @pl.when(i < chunks)
        def _():
            for q in range(classes):
                pl.when((i % classes == q) & (i > 0))(functools.partial(compute, i, q))
            first(i)

        @pl.when((i >= LAG_SECOND) & (i < chunks + LAG_SECOND))
        def _():
            second(i - LAG_SECOND)

        @pl.when(i >= LAG_ROUTE)
        def _():
            route(i - LAG_ROUTE)

        return carry

    compute(0, 0)
    pl.semaphore_wait(barrier, 2 + shards - 1)
    lax.fori_loop(0, chunks + LAG_ROUTE, step, 0)

    def arrive(k, carry):
        source = peer(k)
        for q in range(classes):
            for part in range(slots // run):
                pltpu.make_async_remote_copy(
                    src_ref=s3.at[0, 0], dst_ref=arr.at[q, source, part], send_sem=sem_s3.at[0, 0],
                    recv_sem=sem_r3.at[q, source, part], device_id={"sec": source},
                    device_id_type=MESH).wait_recv()
        return carry

    lax.fori_loop(0, shards - 1, arrive, 0)

    def place(n, carry):
        for u in range(GROUP):
            slot = n * GROUP + u
            total = None
            for q in range(classes):
                at = table_sm[classes + q, slot]
                here = arr[q, at // slots, (at % slots) // run, at % run].astype(jnp.float32)
                total = here if total is None else total + here
            out_ref[slot] = total
        return carry

    lax.fori_loop(0, out_ref.shape[0] // GROUP, place, 0)

    def drain(i, carry):
        for h in range(2):
            first_copy(h, i).wait_send()
            second_copy(h, i).wait_send()
        for e in range(chunk // run):
            at = (i // classes) * chunk + e * run
            k, part = at // slots, (at % slots) // run

            @pl.when(k < shards - 1)
            def _():
                route_copy(i, e, i % classes, k, part).wait_send()
        return carry

    lax.fori_loop(0, chunks, drain, 0)


def per_device(wavefunction, left_ops, right_ops, left_sector, right_sector, target):
    shards, parts = lax.axis_size("sec"), lax.axis_size("op")
    assert parts == 4
    blocks_here, bl, br = wavefunction.shape
    classes = target.shape[0]
    slots = blocks_here // shards
    chunk = min(blocks_here, GROUP)
    chunks = classes * blocks_here // chunk
    run = min(chunk, slots)
    half, rows, dests = chunk // 2, bl // parts, chunk // run
    table = (2 * classes + -2 * classes % 8, blocks_here + -blocks_here % 128)
    smem, vmem = pl.BlockSpec(memory_space=pltpu.SMEM), pl.BlockSpec(memory_space=pltpu.VMEM)
    wide, narrow = jnp.float32, jnp.bfloat16
    flops = 4 * blocks_here * classes * left_ops.shape[1] * bl * bl * br
    return pl.pallas_call(
        functools.partial(kernel, (shards, classes, chunks, chunk, slots)),
        out_shape=jax.ShapeDtypeStruct((blocks_here, rows, br), wide),
        in_specs=[smem] * 2 + [vmem] + [pl.BlockSpec(memory_space=pl.ANY)] * 3,
        out_specs=vmem,
        scratch_shapes=[
            pltpu.VMEM(wavefunction.shape, wavefunction.dtype),
            [pltpu.VMEM(left_ops.shape[1:], left_ops.dtype)] * classes,
            [pltpu.VMEM(right_ops.shape[1:], right_ops.dtype)] * classes,
            pltpu.VMEM(table, jnp.int32),
            pltpu.SMEM(table, jnp.int32),
            pltpu.VMEM((chunks, chunk, parts, rows, br), wide),
            pltpu.VMEM((2, chunks, half, 2, rows, br), narrow),
            pltpu.VMEM((2, chunks, half, 2, rows, br), narrow),
            pltpu.VMEM((2, chunks, half, rows, br), narrow),
            pltpu.VMEM((2, chunks, half, rows, br), narrow),
            pltpu.VMEM((chunks, dests, run, rows, br), narrow),
            pltpu.VMEM((classes, shards, slots // run, run, rows, br), narrow),
            pltpu.SemaphoreType.DMA((2 * classes + 2,)),
            pltpu.SemaphoreType.DMA((2, chunks)),
            pltpu.SemaphoreType.DMA((2, chunks)),
            pltpu.SemaphoreType.DMA((2, chunks)),
            pltpu.SemaphoreType.DMA((2, chunks)),
            pltpu.SemaphoreType.DMA((chunks, dests)),
            pltpu.SemaphoreType.DMA((classes, shards, slots // run)),
        ],
        compiler_params=pltpu.CompilerParams(
            collective_id=0, has_side_effects=True, vmem_limit_bytes=56 * 1024 * 1024),
        cost_estimate=pl.CostEstimate(flops=flops, bytes_accessed=8 * 1024 * 1024, transcendentals=0),
    )(left_sector, right_sector, target, wavefunction, left_ops, right_ops)


def solution(mesh):
    in_specs = (
        P("sec", None, None),
        P(None, "op", None, None, None),
        P(None, "op", None, None, None),
        P("sec"),
        P("sec"),
        P(),
    )
    out_specs = P("sec", "op", None)
    return jax.shard_map(
        per_device, mesh=mesh, in_specs=in_specs, out_specs=out_specs, check_vma=False
    )
```

```python
import functools

import jax
import jax.numpy as jnp
from jax import lax
from jax.experimental import pallas as pl
from jax.experimental.pallas import tpu as pltpu
from jax.sharding import PartitionSpec as P

MESH = pl.DeviceIdType.MESH
GROUP = 8
BESIDE = 4
LAG_SECOND = 3
LAG_ROUTE = 6


def fill_tables(whole_ref, classes, table, me, shards, slots):
    total = whole_ref.shape[1]
    n = total // shards
    table[2 * classes:2 * classes + 2, 0:n] = whole_ref[classes:classes + 2, 0:n]
    block = lax.broadcasted_iota(jnp.int32, (n, total), 1)
    here = me * n + lax.broadcasted_iota(jnp.int32, (n, total), 0)
    row, col = (lax.broadcasted_iota(jnp.int32, (n, n), axis) for axis in range(2))
    bound = (lax.broadcasted_iota(jnp.int32, (n, shards), 1) + 1) * n

    def count(mask):
        return jnp.sum(jnp.where(mask, 1, 0), axis=1, keepdims=True)

    def as_row(column):
        return jnp.sum(jnp.where(row == col, column, 0), axis=0, keepdims=True)

    for q in range(classes):
        target = whole_ref[q:q + 1, :]
        mine = jnp.sum(jnp.where(block == here, target, 0), axis=1, keepdims=True)
        position = count(as_row(mine) < mine)
        order = jnp.sum(jnp.where(position == col, row, 0), axis=0, keepdims=True)
        table[q:q + 1, 0:n] = jnp.minimum(order, n - 1)
        origin = jnp.sum(jnp.where(target == here, block, 0), axis=1, keepdims=True)
        source = count(origin >= bound)
        rank = count((as_row(source) == source) & (col < row))
        table[classes + q:classes + q + 1, 0:n] = jnp.minimum(as_row(source * slots + rank), n - 1)


def kernel(sizes, whole_ref, w_any, l_any, r_any, out_ref,
           w_ref, l_refs, r_refs, table, table_sm, acc, s1, r1, s2, r2, s3, arr,
           sem_in, sem_s1, sem_r1, sem_s2, sem_r2, sem_s3, sem_r3):
    shards, classes, chunks, chunk, slots = sizes
    half = chunk // 2
    terms, bl = l_any.shape[1], l_any.shape[3]
    rows = acc.shape[3]
    op, me = lax.axis_index("op"), lax.axis_index("sec")
    hi, lo = op // 2, op % 2
    own = hi * 2 + lo
    near_lo, near_hi = hi * 2 + 1 - lo, (1 - hi) * 2 + lo
    run = min(chunk, slots)

    def peer(k):
        off = shards // 2 + (1 - 2 * (k % 2)) * ((k + 1) // 2)
        return (me + off + shards) % shards

    pieces = classes * terms
    part = w_ref.shape[0] // pieces
    for u in range(pieces):
        span = pl.ds(u * part, part)
        pltpu.make_async_copy(w_any.at[span], w_ref.at[span], sem_in.at[2 * classes]).start()

    def fetch(q):
        for t in range(terms):
            pltpu.make_async_copy(l_any.at[q, t], l_refs[q].at[t], sem_in.at[q]).start()
            pltpu.make_async_copy(r_any.at[q, t], r_refs[q].at[t], sem_in.at[classes + q]).start()

    def fetched(q):
        pltpu.make_async_copy(l_any.at[q], l_refs[q], sem_in.at[q]).wait()
        pltpu.make_async_copy(r_any.at[q], r_refs[q], sem_in.at[classes + q]).wait()

    fetch(0)

    barrier = pltpu.get_barrier_semaphore()
    for other in (near_lo, near_hi):
        pl.semaphore_signal(barrier, inc=1, device_id={"op": other}, device_id_type=MESH)

    def greet(k, carry):
        pl.semaphore_signal(barrier, inc=1, device_id={"sec": peer(k)}, device_id_type=MESH)
        return carry

    lax.fori_loop(0, shards - 1, greet, 0)
    fill_tables(whole_ref, classes, table, me, shards, slots)
    copy = pltpu.make_async_copy(table, table_sm, sem_in.at[2 * classes + 1])
    copy.start()
    copy.wait()
    pltpu.make_async_copy(w_any, w_ref, sem_in.at[2 * classes]).wait()
    def first_copy(h, i):
        return pltpu.make_async_remote_copy(
            src_ref=s1.at[h, i], dst_ref=r1.at[h, i], send_sem=sem_s1.at[h, i], recv_sem=sem_r1.at[h, i],
            device_id={"op": near_lo if h == 0 else near_hi}, device_id_type=MESH)

    def second_copy(h, i):
        return pltpu.make_async_remote_copy(
            src_ref=s2.at[h, i], dst_ref=r2.at[h, i], send_sem=sem_s2.at[h, i], recv_sem=sem_r2.at[h, i],
            device_id={"op": near_hi if h == 0 else near_lo}, device_id_type=MESH)

    def route_copy(i, e, q, k, part):
        return pltpu.make_async_remote_copy(
            src_ref=s3.at[i, e], dst_ref=arr.at[q, me, part], send_sem=sem_s3.at[i, e],
            recv_sem=sem_r3.at[q, me, part],
            device_id={"sec": peer(k)}, device_id_type=MESH)

    def compute(i, q, h):
        c = i // classes
        if q > 0 and h == 0:
            pl.when(i == q)(functools.partial(fetched, q))
        for start in range(h * half, (h + 1) * half, BESIDE):
            spots = []
            for b in range(start, min(start + BESIDE, (h + 1) * half)):
                place_at = c * chunk + b
                block = table_sm[q, peer(place_at // slots) * slots + place_at % slots]
                spots.append((b, block, table_sm[2 * classes, block], table_sm[2 * classes + 1, block]))
            mixes = []
            for b, block, left, right in spots:
                mixed = jnp.dot(
                    l_refs[q][:, left].reshape(terms * bl, l_any.shape[4]), w_ref[block],
                    preferred_element_type=jnp.float32).astype(jnp.bfloat16)
                mixes.append(jnp.concatenate([mixed[t * bl:(t + 1) * bl] for t in range(terms)], axis=1))
            values = []
            for (b, block, left, right), mixed in zip(spots, mixes):
                rights = jnp.concatenate([r_refs[q][t, right] for t in range(terms)], axis=1)
                values.append(lax.dot_general(
                    mixed, rights, (((1,), (1,)), ((), ())), preferred_element_type=jnp.float32))
            for (b, block, left, right), value in zip(spots, values):
                acc[i, b] = value.reshape(acc.shape[2:])

    def first(i, h):
        for j in range(2):
            away = j * 2 + 1 - lo if h == 0 else (1 - hi) * 2 + j
            s1[h, i, :, j] = acc[i, h * half:(h + 1) * half, away].astype(jnp.bfloat16)
        first_copy(h, i).start()

    def second(i):
        first_copy(0, i).wait_recv()
        s2[0, i] = (acc[i, 0:half, near_hi] + r1[0, i, :, 1 - hi].astype(jnp.float32)).astype(jnp.bfloat16)
        second_copy(0, i).start()
        first_copy(1, i).wait_recv()
        s2[1, i] = (acc[i, half:chunk, near_lo] + r1[1, i, :, 1 - lo].astype(jnp.float32)).astype(jnp.bfloat16)
        second_copy(1, i).start()
        acc[i, 0:half, own] = acc[i, 0:half, own] + r1[0, i, :, hi].astype(jnp.float32)
        acc[i, half:chunk, own] = acc[i, half:chunk, own] + r1[1, i, :, lo].astype(jnp.float32)

    def route(i):
        q, c = i % classes, i // classes
        for h in range(2):
            second_copy(h, i).wait_recv()
            total = acc[i, h * half:(h + 1) * half, own] + r2[h, i].astype(jnp.float32)
            acc[i, h * half:(h + 1) * half, own] = total
        for e in range(chunk // run):
            at = c * chunk + e * run
            k, part = at // slots, (at % slots) // run
            share = acc[i, e * run:(e + 1) * run, own].astype(jnp.bfloat16)

            @pl.when(k < shards - 1)
            def _():
                s3[i, e] = share
                route_copy(i, e, q, k, part).start()

            @pl.when(k == shards - 1)
            def _():
                arr[q, me, part] = share

    def step(i, carry):
        @pl.when(i < chunks)
        def _():
            for h in range(2):
                for q in range(classes):
                    pl.when((i % classes == q) & (i + h > 0))(functools.partial(compute, i, q, h))
                first(i, h)

        @pl.when((i >= LAG_SECOND) & (i < chunks + LAG_SECOND))
        def _():
            second(i - LAG_SECOND)

        @pl.when(i >= LAG_ROUTE)
        def _():
            route(i - LAG_ROUTE)

        return carry

    fetched(0)
    for q in range(1, classes):
        fetch(q)
    compute(0, 0, 0)
    pl.semaphore_wait(barrier, 2 + shards - 1)
    lax.fori_loop(0, chunks + LAG_ROUTE, step, 0)

    def arrive(k, carry):
        source = peer(k)
        for q in range(classes):
            for part in range(slots // run):
                pltpu.make_async_remote_copy(
                    src_ref=s3.at[0, 0], dst_ref=arr.at[q, source, part], send_sem=sem_s3.at[0, 0],
                    recv_sem=sem_r3.at[q, source, part], device_id={"sec": source},
                    device_id_type=MESH).wait_recv()
        return carry

    lax.fori_loop(0, shards - 1, arrive, 0)

    def place(n, carry):
        for u in range(GROUP):
            slot = n * GROUP + u
            total = None
            for q in range(classes):
                at = table_sm[classes + q, slot]
                here = arr[q, at // slots, (at % slots) // run, at % run].astype(jnp.float32)
                total = here if total is None else total + here
            out_ref[slot] = total
        return carry

    lax.fori_loop(0, out_ref.shape[0] // GROUP, place, 0)

    def drain(i, carry):
        for h in range(2):
            first_copy(h, i).wait_send()
            second_copy(h, i).wait_send()
        for e in range(chunk // run):
            at = (i // classes) * chunk + e * run
            k, part = at // slots, (at % slots) // run

            @pl.when(k < shards - 1)
            def _():
                route_copy(i, e, i % classes, k, part).wait_send()
        return carry

    lax.fori_loop(0, chunks, drain, 0)


def per_device(wavefunction, left_ops, right_ops, left_sector, right_sector, target):
    shards, parts = lax.axis_size("sec"), lax.axis_size("op")
    assert parts == 4
    blocks_here, bl, br = wavefunction.shape
    classes = target.shape[0]
    slots = blocks_here // shards
    chunk = min(blocks_here, GROUP)
    chunks = classes * blocks_here // chunk
    run = min(chunk, slots)
    half, rows, dests = chunk // 2, bl // parts, chunk // run
    table = (2 * classes + 2 + (-2 * classes - 2) % 8, blocks_here + -blocks_here % 128)
    vmem = pl.BlockSpec(memory_space=pltpu.VMEM)
    sectors = jnp.pad(jnp.stack([left_sector, right_sector]), ((0, 0), (0, target.shape[1] - blocks_here)))
    whole = jnp.concatenate([target, sectors], axis=0)
    wide, narrow = jnp.float32, jnp.bfloat16
    flops = 4 * blocks_here * classes * left_ops.shape[1] * bl * bl * br
    return pl.pallas_call(
        functools.partial(kernel, (shards, classes, chunks, chunk, slots)),
        out_shape=jax.ShapeDtypeStruct((blocks_here, rows, br), wide),
        in_specs=[vmem] + [pl.BlockSpec(memory_space=pl.ANY)] * 3,
        out_specs=vmem,
        scratch_shapes=[
            pltpu.VMEM(wavefunction.shape, wavefunction.dtype),
            [pltpu.VMEM(left_ops.shape[1:], left_ops.dtype)] * classes,
            [pltpu.VMEM(right_ops.shape[1:], right_ops.dtype)] * classes,
            pltpu.VMEM(table, jnp.int32),
            pltpu.SMEM(table, jnp.int32),
            pltpu.VMEM((chunks, chunk, parts, rows, br), wide),
            pltpu.VMEM((2, chunks, half, 2, rows, br), narrow),
            pltpu.VMEM((2, chunks, half, 2, rows, br), narrow),
            pltpu.VMEM((2, chunks, half, rows, br), narrow),
            pltpu.VMEM((2, chunks, half, rows, br), narrow),
            pltpu.VMEM((chunks, dests, run, rows, br), narrow),
            pltpu.VMEM((classes, shards, slots // run, run, rows, br), narrow),
            pltpu.SemaphoreType.DMA((2 * classes + 2,)),
            pltpu.SemaphoreType.DMA((2, chunks)),
            pltpu.SemaphoreType.DMA((2, chunks)),
            pltpu.SemaphoreType.DMA((2, chunks)),
            pltpu.SemaphoreType.DMA((2, chunks)),
            pltpu.SemaphoreType.DMA((chunks, dests)),
            pltpu.SemaphoreType.DMA((classes, shards, slots // run)),
        ],
        compiler_params=pltpu.CompilerParams(
            collective_id=0, has_side_effects=True, vmem_limit_bytes=52 * 1024 * 1024),
        cost_estimate=pl.CostEstimate(flops=flops, bytes_accessed=8 * 1024 * 1024, transcendentals=0),
    )(whole, wavefunction, left_ops, right_ops)


def solution(mesh):
    in_specs = (
        P("sec", None, None),
        P(None, "op", None, None, None),
        P(None, "op", None, None, None),
        P("sec"),
        P("sec"),
        P(),
    )
    out_specs = P("sec", "op", None)
    return jax.shard_map(
        per_device, mesh=mesh, in_specs=in_specs, out_specs=out_specs, check_vma=False
    )
```

```python
import functools

import jax
import jax.numpy as jnp
from jax import lax
from jax.experimental import pallas as pl
from jax.experimental.pallas import tpu as pltpu
from jax.sharding import PartitionSpec as P

MESH = pl.DeviceIdType.MESH
GROUP = 8
BESIDE = 4
LAG_SECOND = 3
LAG_ROUTE = 6


def fill_tables(whole_ref, classes, table, me, shards, slots):
    total = whole_ref.shape[1]
    n = total // shards
    table[2 * classes:2 * classes + 2, 0:n] = whole_ref[classes:classes + 2, 0:n]
    block = lax.broadcasted_iota(jnp.int32, (n, total), 1)
    here = me * n + lax.broadcasted_iota(jnp.int32, (n, total), 0)
    row, col = (lax.broadcasted_iota(jnp.int32, (n, n), axis) for axis in range(2))
    bound = (lax.broadcasted_iota(jnp.int32, (n, shards), 1) + 1) * n

    def count(mask):
        return jnp.sum(jnp.where(mask, 1, 0), axis=1, keepdims=True)

    def as_row(column):
        return jnp.sum(jnp.where(row == col, column, 0), axis=0, keepdims=True)

    for q in range(classes):
        target = whole_ref[q:q + 1, :]
        mine = jnp.sum(jnp.where(block == here, target, 0), axis=1, keepdims=True)
        position = count(as_row(mine) < mine)
        order = jnp.sum(jnp.where(position == col, row, 0), axis=0, keepdims=True)
        table[q:q + 1, 0:n] = jnp.minimum(order, n - 1)
        origin = jnp.sum(jnp.where(target == here, block, 0), axis=1, keepdims=True)
        source = count(origin >= bound)
        rank = count((as_row(source) == source) & (col < row))
        table[classes + q:classes + q + 1, 0:n] = jnp.minimum(as_row(source * slots + rank), n - 1)


def kernel(sizes, whole_ref, w_any, l_any, r_any, out_ref,
           w_ref, l_refs, r_refs, table, table_sm, acc, s1, r1, s2, r2, s3, arr,
           sem_in, sem_s1, sem_r1, sem_s2, sem_r2, sem_s3, sem_r3):
    shards, classes, chunks, chunk, slots = sizes
    half = chunk // 2
    terms, bl = l_any.shape[1], l_any.shape[3]
    rows = acc.shape[3]
    op, me = lax.axis_index("op"), lax.axis_index("sec")
    hi, lo = op // 2, op % 2
    own = hi * 2 + lo
    near_lo, near_hi = hi * 2 + 1 - lo, (1 - hi) * 2 + lo
    run = min(chunk, slots)

    def peer(k):
        off = shards // 2 + (1 - 2 * (k % 2)) * ((k + 1) // 2)
        return (me + off + shards) % shards

    pieces = classes * terms
    part = w_ref.shape[0] // pieces
    for u in range(pieces):
        span = pl.ds(u * part, part)
        pltpu.make_async_copy(w_any.at[span], w_ref.at[span], sem_in.at[2 * classes]).start()

    def fetch(q):
        for t in range(terms):
            pltpu.make_async_copy(l_any.at[q, t], l_refs[q].at[t], sem_in.at[q]).start()
            pltpu.make_async_copy(r_any.at[q, t], r_refs[q].at[t], sem_in.at[classes + q]).start()

    def fetched(q):
        pltpu.make_async_copy(l_any.at[q], l_refs[q], sem_in.at[q]).wait()
        pltpu.make_async_copy(r_any.at[q], r_refs[q], sem_in.at[classes + q]).wait()

    fetch(0)

    barrier = pltpu.get_barrier_semaphore()
    for other in (near_lo, near_hi):
        pl.semaphore_signal(barrier, inc=1, device_id={"op": other}, device_id_type=MESH)

    def greet(k, carry):
        pl.semaphore_signal(barrier, inc=1, device_id={"sec": peer(k)}, device_id_type=MESH)
        return carry

    lax.fori_loop(0, shards - 1, greet, 0)
    fill_tables(whole_ref, classes, table, me, shards, slots)
    copy = pltpu.make_async_copy(table, table_sm, sem_in.at[2 * classes + 1])
    copy.start()
    copy.wait()
    pltpu.make_async_copy(w_any, w_ref, sem_in.at[2 * classes]).wait()
    def first_copy(h, i):
        return pltpu.make_async_remote_copy(
            src_ref=s1.at[h, i], dst_ref=r1.at[h, i], send_sem=sem_s1.at[h, i], recv_sem=sem_r1.at[h, i],
            device_id={"op": near_lo if h == 0 else near_hi}, device_id_type=MESH)

    def second_copy(h, i):
        return pltpu.make_async_remote_copy(
            src_ref=s2.at[h, i], dst_ref=r2.at[h, i], send_sem=sem_s2.at[h, i], recv_sem=sem_r2.at[h, i],
            device_id={"op": near_hi if h == 0 else near_lo}, device_id_type=MESH)

    def route_copy(i, e, q, k, part):
        return pltpu.make_async_remote_copy(
            src_ref=s3.at[i, e], dst_ref=arr.at[q, me, part], send_sem=sem_s3.at[i, e],
            recv_sem=sem_r3.at[q, me, part],
            device_id={"sec": peer(k)}, device_id_type=MESH)

    def compute(i, q, h):
        c = i // classes
        if q > 0 and h == 0:
            pl.when(i == q)(functools.partial(fetched, q))
        for start in range(h * half, (h + 1) * half, BESIDE):
            spots = []
            for b in range(start, min(start + BESIDE, (h + 1) * half)):
                place_at = c * chunk + b
                block = table_sm[q, peer(place_at // slots) * slots + place_at % slots]
                spots.append((b, block, table_sm[2 * classes, block], table_sm[2 * classes + 1, block]))
            mixes = []
            for b, block, left, right in spots:
                mixed = jnp.dot(
                    l_refs[q][:, left].reshape(terms * bl, l_any.shape[4]), w_ref[block],
                    preferred_element_type=jnp.float32).astype(jnp.bfloat16)
                mixes.append(jnp.concatenate([mixed[t * bl:(t + 1) * bl] for t in range(terms)], axis=1))
            values = []
            for (b, block, left, right), mixed in zip(spots, mixes):
                rights = jnp.concatenate([r_refs[q][t, right] for t in range(terms)], axis=1)
                values.append(lax.dot_general(
                    mixed, rights, (((1,), (1,)), ((), ())), preferred_element_type=jnp.float32))
            for (b, block, left, right), value in zip(spots, values):
                acc[i, b] = value.reshape(acc.shape[2:])

    def first(i, h):
        for j in range(2):
            away = j * 2 + 1 - lo if h == 0 else (1 - hi) * 2 + j
            s1[h, i, :, j] = acc[i, h * half:(h + 1) * half, away].astype(jnp.bfloat16)
        first_copy(h, i).start()

    def second(i):
        first_copy(0, i).wait_recv()
        s2[0, i] = (acc[i, 0:half, near_hi] + r1[0, i, :, 1 - hi].astype(jnp.float32)).astype(jnp.bfloat16)
        second_copy(0, i).start()
        first_copy(1, i).wait_recv()
        s2[1, i] = (acc[i, half:chunk, near_lo] + r1[1, i, :, 1 - lo].astype(jnp.float32)).astype(jnp.bfloat16)
        second_copy(1, i).start()
        acc[i, 0:half, own] = acc[i, 0:half, own] + r1[0, i, :, hi].astype(jnp.float32)
        acc[i, half:chunk, own] = acc[i, half:chunk, own] + r1[1, i, :, lo].astype(jnp.float32)

    def route(i):
        q, c = i % classes, i // classes
        for h in range(2):
            second_copy(h, i).wait_recv()
            total = acc[i, h * half:(h + 1) * half, own] + r2[h, i].astype(jnp.float32)
            acc[i, h * half:(h + 1) * half, own] = total
        for e in range(chunk // run):
            at = c * chunk + e * run
            k, part = at // slots, (at % slots) // run
            share = acc[i, e * run:(e + 1) * run, own].astype(jnp.bfloat16)

            @pl.when(k < shards - 1)
            def _():
                s3[i, e] = share
                route_copy(i, e, q, k, part).start()

            @pl.when(k == shards - 1)
            def _():
                arr[q, me, part] = share

    def step(i, carry):
        @pl.when(i < chunks)
        def _():
            for h in range(2):
                for q in range(classes):
                    pl.when((i % classes == q) & (i + h > 0))(functools.partial(compute, i, q, h))
                first(i, h)

        @pl.when((i >= LAG_SECOND) & (i < chunks + LAG_SECOND))
        def _():
            second(i - LAG_SECOND)

        @pl.when(i >= LAG_ROUTE)
        def _():
            route(i - LAG_ROUTE)

        return carry

    fetched(0)
    for q in range(1, classes):
        fetch(q)
    compute(0, 0, 0)
    pl.semaphore_wait(barrier, 2 + shards - 1)
    lax.fori_loop(0, chunks + LAG_ROUTE, step, 0)

    def arrive(k, carry):
        source = peer(k)
        for q in range(classes):
            for part in range(slots // run):
                pltpu.make_async_remote_copy(
                    src_ref=s3.at[0, 0], dst_ref=arr.at[q, source, part], send_sem=sem_s3.at[0, 0],
                    recv_sem=sem_r3.at[q, source, part], device_id={"sec": source},
                    device_id_type=MESH).wait_recv()
        return carry

    lax.fori_loop(0, shards - 1, arrive, 0)

    def place(n, carry):
        for u in range(GROUP):
            slot = n * GROUP + u
            total = None
            for q in range(classes):
                at = table_sm[classes + q, slot]
                here = arr[q, at // slots, (at % slots) // run, at % run].astype(jnp.float32)
                total = here if total is None else total + here
            out_ref[slot] = total
        return carry

    lax.fori_loop(0, out_ref.shape[0] // GROUP, place, 0)

    def drain(i, carry):
        for h in range(2):
            first_copy(h, i).wait_send()
            second_copy(h, i).wait_send()
        for e in range(chunk // run):
            at = (i // classes) * chunk + e * run
            k, part = at // slots, (at % slots) // run

            @pl.when(k < shards - 1)
            def _():
                route_copy(i, e, i % classes, k, part).wait_send()
        return carry

    lax.fori_loop(0, chunks, drain, 0)


def per_device(wavefunction, left_ops, right_ops, left_sector, right_sector, target):
    shards, parts = lax.axis_size("sec"), lax.axis_size("op")
    assert parts == 4
    blocks_here, bl, br = wavefunction.shape
    classes = target.shape[0]
    slots = blocks_here // shards
    chunk = min(blocks_here, GROUP)
    chunks = classes * blocks_here // chunk
    run = min(chunk, slots)
    half, rows, dests = chunk // 2, bl // parts, chunk // run
    table = (2 * classes + 2 + (-2 * classes - 2) % 8, blocks_here + -blocks_here % 128)
    vmem = pl.BlockSpec(memory_space=pltpu.VMEM)
    rest = target.shape[1] - blocks_here
    whole = jnp.pad(target, ((0, 2), (0, 0)))
    whole += jnp.pad(left_sector[None], ((classes, 1), (0, rest)))
    whole += jnp.pad(right_sector[None], ((classes + 1, 0), (0, rest)))
    wide, narrow = jnp.float32, jnp.bfloat16
    flops = 4 * blocks_here * classes * left_ops.shape[1] * bl * bl * br
    return pl.pallas_call(
        functools.partial(kernel, (shards, classes, chunks, chunk, slots)),
        out_shape=jax.ShapeDtypeStruct((blocks_here, rows, br), wide),
        in_specs=[vmem] + [pl.BlockSpec(memory_space=pl.ANY)] * 3,
        out_specs=vmem,
        scratch_shapes=[
            pltpu.VMEM(wavefunction.shape, wavefunction.dtype),
            [pltpu.VMEM(left_ops.shape[1:], left_ops.dtype)] * classes,
            [pltpu.VMEM(right_ops.shape[1:], right_ops.dtype)] * classes,
            pltpu.VMEM(table, jnp.int32),
            pltpu.SMEM(table, jnp.int32),
            pltpu.VMEM((chunks, chunk, parts, rows, br), wide),
            pltpu.VMEM((2, chunks, half, 2, rows, br), narrow),
            pltpu.VMEM((2, chunks, half, 2, rows, br), narrow),
            pltpu.VMEM((2, chunks, half, rows, br), narrow),
            pltpu.VMEM((2, chunks, half, rows, br), narrow),
            pltpu.VMEM((chunks, dests, run, rows, br), narrow),
            pltpu.VMEM((classes, shards, slots // run, run, rows, br), narrow),
            pltpu.SemaphoreType.DMA((2 * classes + 2,)),
            pltpu.SemaphoreType.DMA((2, chunks)),
            pltpu.SemaphoreType.DMA((2, chunks)),
            pltpu.SemaphoreType.DMA((2, chunks)),
            pltpu.SemaphoreType.DMA((2, chunks)),
            pltpu.SemaphoreType.DMA((chunks, dests)),
            pltpu.SemaphoreType.DMA((classes, shards, slots // run)),
        ],
        compiler_params=pltpu.CompilerParams(
            collective_id=0, has_side_effects=True, vmem_limit_bytes=52 * 1024 * 1024),
        cost_estimate=pl.CostEstimate(flops=flops, bytes_accessed=8 * 1024 * 1024, transcendentals=0),
    )(whole, wavefunction, left_ops, right_ops)


def solution(mesh):
    in_specs = (
        P("sec", None, None),
        P(None, "op", None, None, None),
        P(None, "op", None, None, None),
        P("sec"),
        P("sec"),
        P(),
    )
    out_specs = P("sec", "op", None)
    return jax.shard_map(
        per_device, mesh=mesh, in_specs=in_specs, out_specs=out_specs, check_vma=False
    )
```

```python
import functools

import jax
import jax.numpy as jnp
from jax import lax
from jax.experimental import pallas as pl
from jax.experimental.pallas import tpu as pltpu
from jax.sharding import PartitionSpec as P

MESH = pl.DeviceIdType.MESH
GROUP = 8
BESIDE = 4
LAG_SECOND = 3
LAG_ROUTE = 6


def fill_tables(whole_ref, classes, table, me, shards, slots):
    total = whole_ref.shape[1]
    n = total // shards
    table[2 * classes:2 * classes + 2, 0:n] = whole_ref[classes:classes + 2, 0:n]
    block = lax.broadcasted_iota(jnp.int32, (n, total), 1)
    here = me * n + lax.broadcasted_iota(jnp.int32, (n, total), 0)
    row, col = (lax.broadcasted_iota(jnp.int32, (n, n), axis) for axis in range(2))
    bound = (lax.broadcasted_iota(jnp.int32, (n, shards), 1) + 1) * n

    def count(mask):
        return jnp.sum(jnp.where(mask, 1, 0), axis=1, keepdims=True)

    def as_row(column):
        return jnp.sum(jnp.where(row == col, column, 0), axis=0, keepdims=True)

    for q in range(classes):
        target = whole_ref[q:q + 1, :]
        mine = jnp.sum(jnp.where(block == here, target, 0), axis=1, keepdims=True)
        position = count(as_row(mine) < mine)
        order = jnp.sum(jnp.where(position == col, row, 0), axis=0, keepdims=True)
        table[q:q + 1, 0:n] = jnp.minimum(order, n - 1)
        origin = jnp.sum(jnp.where(target == here, block, 0), axis=1, keepdims=True)
        source = count(origin >= bound)
        rank = count((as_row(source) == source) & (col < row))
        table[classes + q:classes + q + 1, 0:n] = jnp.minimum(as_row(source * slots + rank), n - 1)


def kernel(sizes, whole_ref, w_any, l_any, r_any, out_ref,
           w_ref, l_refs, r_refs, table, table_sm, acc, s1, r1, s2, r2, s3, arr,
           sem_in, sem_s1, sem_r1, sem_s2, sem_r2, sem_s3, sem_r3):
    shards, classes, chunks, chunk, slots = sizes
    half = chunk // 2
    terms, bl = l_any.shape[1], l_any.shape[3]
    rows = acc.shape[3]
    op, me = lax.axis_index("op"), lax.axis_index("sec")
    hi, lo = op // 2, op % 2
    own = hi * 2 + lo
    near_lo, near_hi = hi * 2 + 1 - lo, (1 - hi) * 2 + lo
    run = min(chunk, slots)

    def peer(k):
        off = shards // 2 + (1 - 2 * (k % 2)) * ((k + 1) // 2)
        return (me + off + shards) % shards

    pieces = classes * terms
    part = w_ref.shape[0] // pieces
    for u in range(pieces):
        span = pl.ds(u * part, part)
        pltpu.make_async_copy(w_any.at[span], w_ref.at[span], sem_in.at[2 * classes]).start()

    def fetch(q):
        for t in range(terms):
            pltpu.make_async_copy(l_any.at[q, t], l_refs[q].at[t], sem_in.at[q]).start()
            pltpu.make_async_copy(r_any.at[q, t], r_refs[q].at[t], sem_in.at[classes + q]).start()

    def fetched(q):
        pltpu.make_async_copy(l_any.at[q], l_refs[q], sem_in.at[q]).wait()
        pltpu.make_async_copy(r_any.at[q], r_refs[q], sem_in.at[classes + q]).wait()

    fetch(0)

    barrier = pltpu.get_barrier_semaphore()
    for other in (near_lo, near_hi):
        pl.semaphore_signal(barrier, inc=1, device_id={"op": other}, device_id_type=MESH)

    def greet(k, carry):
        pl.semaphore_signal(barrier, inc=1, device_id={"sec": peer(k)}, device_id_type=MESH)
        return carry

    lax.fori_loop(0, shards - 1, greet, 0)
    fill_tables(whole_ref, classes, table, me, shards, slots)
    copy = pltpu.make_async_copy(table, table_sm, sem_in.at[2 * classes + 1])
    copy.start()
    copy.wait()
    pltpu.make_async_copy(w_any, w_ref, sem_in.at[2 * classes]).wait()
    def first_copy(h, i):
        return pltpu.make_async_remote_copy(
            src_ref=s1.at[h, i], dst_ref=r1.at[h, i], send_sem=sem_s1.at[h, i], recv_sem=sem_r1.at[h, i],
            device_id={"op": near_lo if h == 0 else near_hi}, device_id_type=MESH)

    def second_copy(h, i):
        return pltpu.make_async_remote_copy(
            src_ref=s2.at[h, i], dst_ref=r2.at[h, i], send_sem=sem_s2.at[h, i], recv_sem=sem_r2.at[h, i],
            device_id={"op": near_hi if h == 0 else near_lo}, device_id_type=MESH)

    def route_copy(i, e, q, k, part):
        return pltpu.make_async_remote_copy(
            src_ref=s3.at[i, e], dst_ref=arr.at[q, me, part], send_sem=sem_s3.at[i, e],
            recv_sem=sem_r3.at[q, me, part],
            device_id={"sec": peer(k)}, device_id_type=MESH)

    def compute(i, q, h):
        c = i // classes
        if q > 0 and h == 0:
            pl.when(i == q)(functools.partial(fetched, q))
        for start in range(h * half, (h + 1) * half, BESIDE):
            spots = []
            for b in range(start, min(start + BESIDE, (h + 1) * half)):
                place_at = c * chunk + b
                block = table_sm[q, peer(place_at // slots) * slots + place_at % slots]
                spots.append((b, block, table_sm[2 * classes, block], table_sm[2 * classes + 1, block]))
            mixes = []
            for b, block, left, right in spots:
                mixed = jnp.dot(
                    l_refs[q][:, left].reshape(terms * bl, l_any.shape[4]), w_ref[block],
                    preferred_element_type=jnp.float32).astype(jnp.bfloat16)
                mixes.append(jnp.concatenate([mixed[t * bl:(t + 1) * bl] for t in range(terms)], axis=1))
            values = []
            for (b, block, left, right), mixed in zip(spots, mixes):
                rights = jnp.concatenate([r_refs[q][t, right] for t in range(terms)], axis=1)
                values.append(lax.dot_general(
                    mixed, rights, (((1,), (1,)), ((), ())), preferred_element_type=jnp.float32))
            for (b, block, left, right), value in zip(spots, values):
                acc[i, b] = value.reshape(acc.shape[2:])

    def first(i, h):
        for j in range(2):
            away = j * 2 + 1 - lo if h == 0 else (1 - hi) * 2 + j
            s1[h, i, :, j] = acc[i, h * half:(h + 1) * half, away].astype(jnp.bfloat16)
        first_copy(h, i).start()

    def second(i):
        first_copy(0, i).wait_recv()
        s2[0, i] = (acc[i, 0:half, near_hi] + r1[0, i, :, 1 - hi].astype(jnp.float32)).astype(jnp.bfloat16)
        second_copy(0, i).start()
        first_copy(1, i).wait_recv()
        s2[1, i] = (acc[i, half:chunk, near_lo] + r1[1, i, :, 1 - lo].astype(jnp.float32)).astype(jnp.bfloat16)
        second_copy(1, i).start()
        acc[i, 0:half, own] = acc[i, 0:half, own] + r1[0, i, :, hi].astype(jnp.float32)
        acc[i, half:chunk, own] = acc[i, half:chunk, own] + r1[1, i, :, lo].astype(jnp.float32)

    def route(i):
        q, c = i % classes, i // classes
        for h in range(2):
            second_copy(h, i).wait_recv()
            total = acc[i, h * half:(h + 1) * half, own] + r2[h, i].astype(jnp.float32)
            acc[i, h * half:(h + 1) * half, own] = total
        for e in range(chunk // run):
            at = c * chunk + e * run
            k, part = at // slots, (at % slots) // run
            share = acc[i, e * run:(e + 1) * run, own].astype(jnp.bfloat16)

            @pl.when(k < shards - 1)
            def _():
                s3[i, e] = share
                route_copy(i, e, q, k, part).start()

            @pl.when(k == shards - 1)
            def _():
                arr[q, me, part] = share

    def step(i, carry):
        @pl.when((i >= LAG_SECOND) & (i < chunks + LAG_SECOND))
        def _():
            second(i - LAG_SECOND)

        @pl.when(i >= LAG_ROUTE)
        def _():
            route(i - LAG_ROUTE)

        @pl.when(i < chunks)
        def _():
            for h in range(2):
                for q in range(classes):
                    pl.when((i % classes == q) & (i + h > 0))(functools.partial(compute, i, q, h))
                first(i, h)

        return carry

    fetched(0)
    for q in range(1, classes):
        fetch(q)
    compute(0, 0, 0)
    pl.semaphore_wait(barrier, 2 + shards - 1)
    lax.fori_loop(0, chunks + LAG_ROUTE, step, 0)

    def arrive(k, carry):
        source = peer(k)
        for q in range(classes):
            for part in range(slots // run):
                pltpu.make_async_remote_copy(
                    src_ref=s3.at[0, 0], dst_ref=arr.at[q, source, part], send_sem=sem_s3.at[0, 0],
                    recv_sem=sem_r3.at[q, source, part], device_id={"sec": source},
                    device_id_type=MESH).wait_recv()
        return carry

    lax.fori_loop(0, shards - 1, arrive, 0)

    def place(n, carry):
        for u in range(GROUP):
            slot = n * GROUP + u
            total = None
            for q in range(classes):
                at = table_sm[classes + q, slot]
                here = arr[q, at // slots, (at % slots) // run, at % run].astype(jnp.float32)
                total = here if total is None else total + here
            out_ref[slot] = total
        return carry

    lax.fori_loop(0, out_ref.shape[0] // GROUP, place, 0)

    def drain(i, carry):
        for h in range(2):
            first_copy(h, i).wait_send()
            second_copy(h, i).wait_send()
        for e in range(chunk // run):
            at = (i // classes) * chunk + e * run
            k, part = at // slots, (at % slots) // run

            @pl.when(k < shards - 1)
            def _():
                route_copy(i, e, i % classes, k, part).wait_send()
        return carry

    lax.fori_loop(0, chunks, drain, 0)


def per_device(wavefunction, left_ops, right_ops, left_sector, right_sector, target):
    shards, parts = lax.axis_size("sec"), lax.axis_size("op")
    assert parts == 4
    blocks_here, bl, br = wavefunction.shape
    classes = target.shape[0]
    slots = blocks_here // shards
    chunk = min(blocks_here, GROUP)
    chunks = classes * blocks_here // chunk
    run = min(chunk, slots)
    half, rows, dests = chunk // 2, bl // parts, chunk // run
    table = (2 * classes + 2 + (-2 * classes - 2) % 8, blocks_here + -blocks_here % 128)
    vmem = pl.BlockSpec(memory_space=pltpu.VMEM)
    rest = target.shape[1] - blocks_here
    whole = jnp.pad(target, ((0, 2), (0, 0)))
    whole += jnp.pad(left_sector[None], ((classes, 1), (0, rest)))
    whole += jnp.pad(right_sector[None], ((classes + 1, 0), (0, rest)))
    wide, narrow = jnp.float32, jnp.bfloat16
    flops = 4 * blocks_here * classes * left_ops.shape[1] * bl * bl * br
    return pl.pallas_call(
        functools.partial(kernel, (shards, classes, chunks, chunk, slots)),
        out_shape=jax.ShapeDtypeStruct((blocks_here, rows, br), wide),
        in_specs=[vmem] + [pl.BlockSpec(memory_space=pl.ANY)] * 3,
        out_specs=vmem,
        scratch_shapes=[
            pltpu.VMEM(wavefunction.shape, wavefunction.dtype),
            [pltpu.VMEM(left_ops.shape[1:], left_ops.dtype)] * classes,
            [pltpu.VMEM(right_ops.shape[1:], right_ops.dtype)] * classes,
            pltpu.VMEM(table, jnp.int32),
            pltpu.SMEM(table, jnp.int32),
            pltpu.VMEM((chunks, chunk, parts, rows, br), wide),
            pltpu.VMEM((2, chunks, half, 2, rows, br), narrow),
            pltpu.VMEM((2, chunks, half, 2, rows, br), narrow),
            pltpu.VMEM((2, chunks, half, rows, br), narrow),
            pltpu.VMEM((2, chunks, half, rows, br), narrow),
            pltpu.VMEM((chunks, dests, run, rows, br), narrow),
            pltpu.VMEM((classes, shards, slots // run, run, rows, br), narrow),
            pltpu.SemaphoreType.DMA((2 * classes + 2,)),
            pltpu.SemaphoreType.DMA((2, chunks)),
            pltpu.SemaphoreType.DMA((2, chunks)),
            pltpu.SemaphoreType.DMA((2, chunks)),
            pltpu.SemaphoreType.DMA((2, chunks)),
            pltpu.SemaphoreType.DMA((chunks, dests)),
            pltpu.SemaphoreType.DMA((classes, shards, slots // run)),
        ],
        compiler_params=pltpu.CompilerParams(
            collective_id=0, has_side_effects=True, vmem_limit_bytes=52 * 1024 * 1024),
        cost_estimate=pl.CostEstimate(flops=flops, bytes_accessed=8 * 1024 * 1024, transcendentals=0),
    )(whole, wavefunction, left_ops, right_ops)


def solution(mesh):
    in_specs = (
        P("sec", None, None),
        P(None, "op", None, None, None),
        P(None, "op", None, None, None),
        P("sec"),
        P("sec"),
        P(),
    )
    out_specs = P("sec", "op", None)
    return jax.shard_map(
        per_device, mesh=mesh, in_specs=in_specs, out_specs=out_specs, check_vma=False
    )
```
